512 devices in a mesh: dom: 32 (over x, z_hi, core), orient: 16 (over y, z_lo).
Axes of the slice: x: 4, y: 8, z: 8 (z_hi: 4, z_lo: 2; z = z_hi * 2 + z_lo), core: 2. Of those that a mesh axis runs over, the one named last changes fastest.
Arguments:
- images: bfloat16 [512, 2, 8192], P('dom')
- slices: bfloat16 [1024, 2, 8192], P(('orient', 'dom'))
- noise_weight: float32 [8192], replicated, may hold values from 0.2 to 5
- shifts: int32 [49, 2], replicated, may hold values from -3 to 3, as said below
- kernels: bfloat16 [64, 128, 128], replicated, may hold values from -0.5 to 0.5
- targets: int32 [1024, 64], P('orient'), may hold values from 0 to 1535
Outputs:
- volume: float32 [1536, 2, 128], P(('dom', 'orient'))
- loglik: float32 [512], P('dom')
The draws below stay inside these ranges and needn't reach their ends.
Inputs may be any that keep to these rules, and one draw needn't show every extreme that they name: `shifts`: translation 0 is the zero shift.
All inputs are finite; a program needn't handle non-finite values.
Results may differ from the reference program's by a relative error of at most 0.0059.
Values may be sent and summed in bfloat16 or wider, within the bound.
A program may use at most 64 MiB of HBM per device.

```python
import math
import jax
import jax.numpy as jnp
from jax import lax

PIX = 8192
TRANS = 49
BLOCK_PIX = 128
BLOCK_VOX = 128
PIX_BLOCKS = 64
ORIENTS = 1024
IMAGES = 512
VOL_BLOCKS = 1536


def common_slices(key):
    return jax.random.normal(key, (ORIENTS, 2, PIX), jnp.float32) * (2.0 * PIX) ** (-0.5)


def draw_slices(key, part):
    return common_slices(key).astype(jnp.bfloat16)


def draw_images(key, part):
    key = jax.random.fold_in(key, 2)
    noise = jax.random.normal(jax.random.fold_in(key, 1), (IMAGES, 2, PIX), jnp.float32)
    return noise.astype(jnp.bfloat16)


def draw_shifts(key, part):
    key = jax.random.fold_in(key, 5)
    moved = jax.random.randint(key, (TRANS, 2), -3, 4)
    row = jnp.arange(TRANS, dtype=jnp.int32)[:, None]
    edge = jnp.where(row == 1, jnp.array([[3, -3]], jnp.int32), moved)
    return jnp.where(row == 0, 0, edge).astype(jnp.int32)


def place_ends(values, own_key, least, top_value):
    longest = values.shape.index(max(values.shape))
    spots = []
    for shift in (0, 1):
        where = [jax.random.randint(jax.random.fold_in(own_key, axis), (), 0, length) for axis, length in enumerate(values.shape)]
        where[longest] = (where[longest] + shift) % values.shape[longest]
        spots.append(tuple(where))
    return values.at[spots[0]].set(least).at[spots[1]].set(top_value)


def gaussian(key, extent, scale, limit, kind=jnp.bfloat16):
    entries = scale * jax.random.normal(key, extent, jnp.float32)
    return jnp.clip(entries, min=-limit, max=limit).astype(kind)


def setup_inputs(seed: int = 0) -> dict:
    arg_keys = jax.random.split(jax.random.key(seed), 7)
    images = draw_images(jax.random.fold_in(arg_keys[6], 71), 0)
    slices = draw_slices(jax.random.fold_in(arg_keys[6], 71), 0)
    noise_weight = jnp.clip(jnp.exp(jax.random.uniform(arg_keys[2], (PIX,), jnp.float32, math.log(0.2), math.log(5.0))), 0.2, 5.0)
    shifts = draw_shifts(jax.random.fold_in(arg_keys[6], 71), 0)
    kernels = gaussian(arg_keys[4], (PIX_BLOCKS, BLOCK_PIX, BLOCK_VOX), BLOCK_PIX ** -0.5, 0.5)
    targets = place_ends(jax.random.randint(arg_keys[5], (ORIENTS, PIX_BLOCKS), 0, VOL_BLOCKS), jax.random.fold_in(arg_keys[5], 1), 0, VOL_BLOCKS - 1).astype(jnp.int32)
    return dict(images=images, slices=slices, noise_weight=noise_weight, shifts=shifts, kernels=kernels, targets=targets)


def phase_table(shift_rows):
    comp = jnp.arange(PIX, dtype=jnp.int32)
    freq_x = (comp % 64).astype(jnp.float32)
    freq_y = (comp // 64 - PIX // 128).astype(jnp.float32)
    moved = shift_rows.astype(jnp.float32)
    angle = 2.0 * jnp.pi * (moved[:, 0:1] * freq_x[None, :] + moved[:, 1:2] * freq_y[None, :]) / 128.0
    return jnp.cos(angle), jnp.sin(angle)


def align_images(images, shift_rows, noise_weight):
    cosine, sine = phase_table(shift_rows)
    real_part = images[:, 0, :].astype(jnp.float32)[:, None, :]
    imag_part = images[:, 1, :].astype(jnp.float32)[:, None, :]
    out_real = noise_weight * (real_part * cosine - imag_part * sine)
    out_imag = noise_weight * (real_part * sine + imag_part * cosine)
    return jnp.stack([out_real, out_imag], axis=2).astype(jnp.bfloat16)


def reference(images, slices, noise_weight, shifts, kernels, targets):
    flat_slices = slices.reshape(ORIENTS, 2 * PIX)
    energy = 0.5 * jnp.sum(noise_weight * jnp.square(slices.astype(jnp.float32)), axis=(1, 2))
    group_img = 16
    image_groups = images.reshape(IMAGES // group_img, group_img, 2, PIX)

    def one_block(accum, block):
        aligned = align_images(block, shifts, noise_weight).reshape(group_img * TRANS, 2 * PIX)
        scores = jnp.dot(aligned, flat_slices.T, preferred_element_type=jnp.float32) - energy[None, :]
        scores = scores.reshape(group_img, TRANS * ORIENTS)
        peak = jnp.max(scores, axis=1)
        expo = jnp.exp(scores - peak[:, None])
        mass = jnp.sum(expo, axis=1)
        loglik = peak + jnp.log(mass)
        posterior = (expo / mass[:, None]).astype(jnp.bfloat16).reshape(group_img * TRANS, ORIENTS)
        accum = accum + jnp.dot(posterior.T, aligned, preferred_element_type=jnp.float32)
        return accum, loglik

    accum, logs = lax.scan(one_block, jnp.zeros((ORIENTS, 2 * PIX), jnp.float32), image_groups)
    loglik = logs.reshape(IMAGES)
    blocked = accum.reshape(ORIENTS, 2, PIX_BLOCKS, BLOCK_PIX)
    inserted = jnp.einsum("ocbp,bpq->obcq", blocked, kernels.astype(jnp.float32), precision=lax.Precision.HIGHEST)
    inserted = inserted.reshape(ORIENTS * PIX_BLOCKS, 2 * BLOCK_VOX)
    volume = jax.ops.segment_sum(inserted, targets.reshape(-1).astype(jnp.int32), num_segments=VOL_BLOCKS)
    return volume.reshape(VOL_BLOCKS, 2, BLOCK_VOX), loglik
```

```python
import functools

import jax
import jax.numpy as jnp
import numpy as np
from jax import lax
from jax.experimental import pallas as pl
from jax.experimental.pallas import tpu as pltpu
from jax.sharding import PartitionSpec as P

F32 = jnp.float32
BF16 = jnp.bfloat16
MESH = pl.DeviceIdType.MESH
PIX = 8192
TRANS = 49
FREQ = 64
IMGS = 32
ORI = 32
STEPS = FREQ + 1
VMEM_LIMIT = 56 * 1024 * 1024


def vmem(count):
    return [pl.BlockSpec(memory_space=pltpu.VMEM)] * count


def params(**kw):
    return pltpu.CompilerParams(vmem_limit_bytes=VMEM_LIMIT, **kw)


def tables():
    kx = np.arange(64)
    unit = 2.0 * np.pi / 128.0
    rows = np.zeros((8, 128), np.float32)
    for a in range(4):
        rows[a, :64] = rows[a, 64:] = np.cos(unit * a * kx)
    for a in range(1, 4):
        rows[4 + a, :64] = np.sin(unit * a * kx)
        rows[4 + a, 64:] = -np.sin(unit * a * kx)
    m = np.arange(STEPS)
    sums = np.zeros((STEPS, 8, 128), np.float32)
    for b in range(4):
        sums[:, b, :] = np.cos(unit * b * m)[:, None]
        sums[:, 4 + b, :] = np.where(m == 64, 0.0, np.sin(unit * b * m))[:, None]
    return rows, sums


def fold_kernel(raw_ref, images_ref, slices_ref, rows):
    low = lax.broadcasted_iota(jnp.int32, (18, 128), 1) < 64
    for m in range(FREQ):
        for c in range(2):
            def block(b):
                return raw_ref[:, c * PIX + b * 128 : c * PIX + b * 128 + 128].astype(F32)

            if m % 2 == 0:
                first = block(32 + m // 2)
                second = pltpu.roll(block(32 - m // 2 if m else 0), 64, 1)
            else:
                first = pltpu.roll(block(32 + (m - 1) // 2), 64, 1)
                second = block(32 - (m + 1) // 2)
            both = jnp.where(low, first, second)
            lanes = slice(c * 128, c * 128 + 128)
            images_ref[m, :, lanes] = both[:16].astype(BF16)
            rows[0, m : m + 1, lanes] = both[16:17]
            rows[1, m : m + 1, lanes] = both[17:18]
    slices_ref[...] = rows[...].astype(BF16)


def place():
    dom = lax.axis_index("dom")
    ori = lax.axis_index("orient")
    core = dom % 2
    z_hi = (dom // 2) % 4
    x = dom // 8
    return x, z_hi, core, ori


def gather_kernel(own_images, own_slices, images, slices, send, recv, local):
    x, zh, c, ori = place()

    def dev(xx, zz, cc):
        return (lax.rem(xx + 4, 4) * 8 + lax.rem(zz + 4, 4) * 2 + cc, ori)

    def slot(dx, dz):
        return lax.rem(x + dx, 4) * 4 + lax.rem(zh + dz, 4)

    other = dev(x, zh, 1 - c)
    z_up, z_down = dev(x, zh + 1, c), dev(x, zh - 1, c)
    x_up, x_down = dev(x + 1, zh, c), dev(x - 1, zh, c)
    barrier = pltpu.get_barrier_semaphore()
    for peer in (other, z_up, z_down, x_up, x_down):
        pl.semaphore_signal(barrier, inc=1, device_id=peer, device_id_type=MESH)
    pl.semaphore_wait(barrier, 5)

    sends = []

    def put(src, dst, sem, peer):
        copy = pltpu.make_async_remote_copy(
            src_ref=src, dst_ref=dst, send_sem=send.at[len(sends)], recv_sem=recv.at[sem],
            device_id=peer, device_id_type=MESH,
        )
        copy.start()
        sends.append(copy)

    def got(ref, sem):
        pltpu.make_async_remote_copy(
            src_ref=ref, dst_ref=ref, send_sem=send.at[0], recv_sem=recv.at[sem],
            device_id=other, device_id_type=MESH,
        ).wait_recv()

    home = slot(0, 0)
    put(own_slices, slices.at[home], 0, z_up)
    put(own_slices, slices.at[home], 1, z_down)
    put(own_slices, slices.at[home], 4, x_up)
    put(own_slices, slices.at[home], 5, x_down)
    img = pl.ds(pl.multiple_of(c * 16, 16), 16)
    put(own_images, images.at[:, img], 20, other)
    keep = pltpu.make_async_copy(own_slices, slices.at[home], local.at[0])
    keep.start()
    keep_images = pltpu.make_async_copy(own_images, images.at[:, img], local.at[1])
    keep_images.start()

    def along_x(dz):
        here = slices.at[slot(0, dz)]
        put(here, here, 4 + 4 * dz, x_up)
        put(here, here, 5 + 4 * dz, x_down)

    def pass_x(dz):
        below = slices.at[slot(3, dz)]
        got(below, 4 + 4 * dz)
        put(below.at[0], below.at[0], 6 + 4 * dz, x_up)
        above = slices.at[slot(1, dz)]
        got(above, 5 + 4 * dz)
        put(above.at[1], above.at[1], 7 + 4 * dz, x_down)

    below = slices.at[slot(0, 3)]
    got(below, 0)
    put(below.at[0], below.at[0], 2, z_up)
    along_x(3)
    above = slices.at[slot(0, 1)]
    got(above, 1)
    put(above.at[1], above.at[1], 3, z_down)
    along_x(1)
    pass_x(0)
    far = slices.at[slot(0, 2)]
    got(far.at[0], 2)
    got(far.at[1], 3)
    along_x(2)
    for dz in (3, 1, 2):
        pass_x(dz)
    for dz in range(4):
        far = slices.at[slot(2, dz)]
        got(far.at[0], 6 + 4 * dz)
        got(far.at[1], 7 + 4 * dz)
    got(images.at[:, pl.ds(pl.multiple_of((1 - c) * 16, 16), 16)], 20)
    keep.wait()
    keep_images.wait()
    for copy in sends:
        copy.wait_send()


def gather(images, slices):
    return pl.pallas_call(
        gather_kernel,
        out_shape=(
            jax.ShapeDtypeStruct((FREQ, IMGS, 256), BF16),
            jax.ShapeDtypeStruct((16, 2, FREQ, 256), BF16),
        ),
        in_specs=vmem(2),
        out_specs=vmem(2),
        scratch_shapes=[
            pltpu.SemaphoreType.DMA((21,)),
            pltpu.SemaphoreType.DMA((21,)),
            pltpu.SemaphoreType.DMA((2,)),
        ],
        compiler_params=params(collective_id=0, has_side_effects=True),
        name="gather_slices",
    )(images, slices)


def aligned_rows(pair, factors):
    real, imag = pair[:, :128], pair[:, 128:]
    rows = []
    for r in range(8):
        row = factors[r : r + 1]
        if r == 4:
            rows.append(jnp.zeros((IMGS, 256), F32))
        else:
            rows.append(jnp.concatenate([real * row, imag * row], axis=1))
    return rows


def scores_kernel(
    slices, images, weight, trig, sums, counts, expo_ref, stats_ref, real, imag, acc, energy
):
    sign = jnp.where(lax.broadcasted_iota(jnp.int32, (1, 128), 1) < 64, 1.0, -1.0).astype(F32)

    def widen(o, carry):
        block = slices[o].astype(F32)
        rows = pl.ds(pl.multiple_of(o * FREQ, FREQ), FREQ)
        real[rows, :] = block[:, :128]
        imag[rows, :] = block[:, 128:]
        return carry

    lax.fori_loop(0, ORI, widen, 0)
    acc[...] = jnp.zeros_like(acc)
    energy[...] = jnp.zeros_like(energy)

    def correlate(m, src):
        at = pl.ds(src, ORI, stride=FREQ)
        s_r, s_i = real[at, :], imag[at, :]
        w = weight[pl.ds(m, 1), :]
        energy[...] += w * (s_r * s_r + s_i * s_i)
        left = jnp.concatenate(
            [
                jnp.concatenate([s_r, s_i], axis=1),
                jnp.concatenate([-sign * s_i, sign * s_r], axis=1),
            ],
            axis=0,
        ).astype(BF16)
        rows = aligned_rows(images[src].astype(F32), trig[...] * w)
        high = [row.astype(BF16) for row in rows]
        low = [(row - top.astype(F32)).astype(BF16) for row, top in zip(rows, high)]
        dims = (((1,), (1,)), ((), ()))
        return lax.dot_general(
            left, jnp.concatenate(high, axis=0), dims, preferred_element_type=F32
        ) + lax.dot_general(left, jnp.concatenate(low, axis=0), dims, preferred_element_type=F32)

    def some(group, carry):
        parts = []
        for j in range(5):
            m = group * 5 + j
            parts.append((m, correlate(m, lax.rem(m, FREQ))))
        for b in range(4):
            for c in range(2):
                for half in range(2):
                    even = c == half
                    if b == 0 and not even:
                        continue
                    lanes = slice(half * 128, half * 128 + 128)
                    total = acc[b, c * ORI : (c + 1) * ORI, lanes]
                    for m, part in parts:
                        value = part[c * ORI : (c + 1) * ORI, lanes]
                        if b:
                            value = value * sums[m, pl.ds(b if even else 4 + b, 1), :]
                        total = total + value
                    acc[b, c * ORI : (c + 1) * ORI, lanes] = total
        return carry

    lax.fori_loop(0, STEPS // 5, some, 0)
    half_energy = 0.5 * jnp.sum(energy[...], axis=1, keepdims=True)
    peak = jnp.full((ORI, 128), -1e30, F32)
    for b in range(4):
        q1 = acc[b, :ORI, :128] - half_energy
        q2 = acc[b, :ORI, 128:]
        q4 = acc[b, ORI:, :128]
        q3 = acc[b, ORI:, 128:]
        for tau in (1, -1) if b else (1,):
            for sigma in (1, -1):
                entry = entry_of(sigma, tau * b)
                value = q1 - sigma * q3
                if b:
                    value = value - tau * (sigma * q2 + q4)
                expo_ref[entry] = value
                peak = jnp.maximum(peak, jnp.where(counts[pl.ds(entry, 1), :] > 0, value, -1e30))
    peak = jnp.max(peak, axis=0, keepdims=True)
    peak = jnp.maximum(peak, pltpu.roll(peak, 32, 1))
    peak = jnp.maximum(peak, pltpu.roll(peak, 64, 1))
    mass = jnp.zeros((ORI, 128), F32)
    for entry in range(14):
        count = counts[pl.ds(entry, 1), :]
        value = jnp.where(count > 0, expo_ref[entry] - peak, -1e30)
        value = jnp.exp(value) * count
        expo_ref[entry] = value
        mass = mass + value
    mass = jnp.sum(mass, axis=0, keepdims=True)
    mass = mass + pltpu.roll(mass, 32, 1)
    mass = mass + pltpu.roll(mass, 64, 1)
    stats_ref[...] = jnp.concatenate([peak, mass, jnp.zeros((6, 128), F32)], axis=0)


def entry_of(sigma, shift_y):
    return (0 if sigma > 0 else 7) + shift_y + 3


def scores(slices, images, weight, trig, sums, counts):
    return pl.pallas_call(
        scores_kernel,
        out_shape=(
            jax.ShapeDtypeStruct((14, ORI, 128), F32),
            jax.ShapeDtypeStruct((8, 128), F32),
        ),
        in_specs=vmem(6),
        out_specs=vmem(2),
        scratch_shapes=[
            pltpu.VMEM((ORI * FREQ, 128), F32),
            pltpu.VMEM((ORI * FREQ, 128), F32),
            pltpu.VMEM((4, 2 * ORI, 256), F32),
            pltpu.VMEM((ORI, 128), F32),
        ],
        compiler_params=params(),
        name="score_images",
    )(slices, images, weight, trig, sums, counts)


def stats_kernel(own, every, send, recv, local):
    x, zh, c, ori = place()
    me = ori * 2 + c

    def dev(index):
        return (x * 8 + zh * 2 + index % 2, index // 2)

    barrier = pltpu.get_barrier_semaphore()
    for step in range(1, 32):
        peer = dev(lax.rem(me + step, 32))
        pl.semaphore_signal(barrier, inc=1, device_id=peer, device_id_type=MESH)
    keep = pltpu.make_async_copy(own, every.at[0], local)
    keep.start()
    pl.semaphore_wait(barrier, 31)
    copies = []
    for step in range(1, 32):
        copies.append(
            pltpu.make_async_remote_copy(
                src_ref=own, dst_ref=every.at[step], send_sem=send.at[step],
                recv_sem=recv.at[step], device_id=dev(lax.rem(me + step, 32)), device_id_type=MESH,
            )
        )
        copies[-1].start()
    keep.wait()
    for copy in copies:
        copy.wait()


def exchange(stats):
    return pl.pallas_call(
        stats_kernel,
        out_shape=jax.ShapeDtypeStruct((32, 8, 128), F32),
        in_specs=vmem(1),
        out_specs=pl.BlockSpec(memory_space=pltpu.VMEM),
        scratch_shapes=[
            pltpu.SemaphoreType.DMA((32,)),
            pltpu.SemaphoreType.DMA((32,)),
            pltpu.SemaphoreType.DMA,
        ],
        compiler_params=params(collective_id=1, has_side_effects=True),
        name="exchange_stats",
    )(stats)


def insert_kernel(
    every, expo, images, weight, trig, sums, kernels, codes,
    volume_ref, loglik_ref, post, folded, inserted, chosen,
):
    sign = jnp.where(lax.broadcasted_iota(jnp.int32, (1, 128), 1) < 64, 1.0, -1.0).astype(F32)
    low = lax.broadcasted_iota(jnp.int32, (2 * ORI, 128), 1) < 64

    place_row = lax.broadcasted_iota(jnp.int32, (512, 128), 0)

    def choose(k, carry):
        for j in range(16):
            hit = place_row == codes[pl.ds(j, 1), :] - k * 512
            rows = pl.ds(pl.multiple_of(k * 512, 512), 512)
            chosen[rows, j * 128 : j * 128 + 128] = jnp.where(hit, 1.0, 0.0).astype(BF16)
        return carry

    lax.fori_loop(0, 3, choose, 0)

    peaks, masses = every[:, 0, :], every[:, 1, :]
    peak = jnp.max(peaks, axis=0, keepdims=True)
    mass = jnp.sum(masses * jnp.exp(peaks - peak), axis=0, keepdims=True)
    loglik_ref[...] = jnp.broadcast_to(peak + jnp.log(mass), (8, 128))
    scale = jnp.exp(peaks[0:1] - peak) / mass
    for b in range(4):
        q1 = jnp.zeros((ORI, 128), F32)
        q2, q3, q4 = q1, q1, q1
        for tau in (1, -1) if b else (1,):
            for sigma in (1, -1):
                value = expo[entry_of(sigma, tau * b)] * scale
                q1 = q1 + value
                q2 = q2 - (sigma * tau) * value
                q3 = q3 - sigma * value
                q4 = q4 - tau * value
        post[b, :ORI, :128] = q1
        post[b, :ORI, 128:] = q2
        post[b, ORI:, :128] = q4
        post[b, ORI:, 128:] = q3

    def back(m, src):
        w = weight[pl.ds(m, 1), :]
        rows = aligned_rows(images[src].astype(F32), trig[...] * w)
        right = jnp.concatenate([row.astype(BF16) for row in rows], axis=0)
        parts = []
        for c in range(2):
            halves = []
            for half in range(2):
                even = c == half
                lanes = slice(half * 128, half * 128 + 128)
                total = None
                for b in range(4):
                    if b == 0 and not even:
                        continue
                    value = post[b, c * ORI : (c + 1) * ORI, lanes]
                    if b:
                        value = value * sums[m, pl.ds(b if even else 4 + b, 1), :]
                    total = value if total is None else total + value
                halves.append(total)
            parts.append(jnp.concatenate(halves, axis=1))
        left = jnp.concatenate(parts, axis=0).astype(BF16)
        grad = jnp.dot(left, right, preferred_element_type=F32)
        real = grad[:ORI, :128] + sign * grad[ORI:, 128:]
        imag = grad[:ORI, 128:] - sign * grad[ORI:, :128]
        return jnp.concatenate([real, imag], axis=0)

    def some_back(group, carry):
        for j in range(4):
            m = group * 4 + j
            folded[m] = back(m, m)
        return carry

    lax.fori_loop(0, FREQ // 4, some_back, 0)
    folded[0] = folded[0] + back(FREQ, 0)

    def insert(block, first, second):
        value = jnp.where(low, first, second)
        high = value.astype(BF16)
        rest = (value - high.astype(F32)).astype(BF16)
        out = jnp.dot(
            jnp.concatenate([high, rest], axis=0), kernels[block], preferred_element_type=F32
        )
        out = out[: 2 * ORI] + out[2 * ORI :]
        rows = pl.ds(pl.multiple_of(block * ORI, ORI), ORI)
        inserted[rows, :] = jnp.concatenate([out[:ORI], out[ORI:]], axis=1).astype(BF16)

    def some_insert(group, carry):
        for j in range(2):
            b = group * 2 + j
            insert(32 + b, folded[2 * b], pltpu.roll(folded[2 * b + 1], 64, 1))
            m = FREQ - 2 * b
            insert(b, pltpu.roll(folded[lax.rem(m, FREQ)], 64, 1), folded[m - 1])
        return carry

    lax.fori_loop(0, 16, some_insert, 0)

    def total(t, carry):
        k, part = t // 2, t % 2
        rows = pl.ds(pl.multiple_of(t * 256, 256), 256)
        sums_here = jnp.dot(chosen[rows, :], inserted[...], preferred_element_type=F32)
        volume_ref[k, pl.ds(pl.multiple_of(part * 256, 256), 256), :] = sums_here
        return carry

    lax.fori_loop(0, 6, total, 0)


def insert(every, expo, images, weight, trig, sums, kernels, codes):
    return pl.pallas_call(
        insert_kernel,
        out_shape=(
            jax.ShapeDtypeStruct((3, 512, 256), F32),
            jax.ShapeDtypeStruct((8, 128), F32),
        ),
        in_specs=vmem(8),
        out_specs=vmem(2),
        scratch_shapes=[
            pltpu.VMEM((4, 2 * ORI, 256), F32),
            pltpu.VMEM((FREQ, 2 * ORI, 128), F32),
            pltpu.VMEM((FREQ * ORI, 256), BF16),
            pltpu.VMEM((1536, 2048), BF16),
        ],
        compiler_params=params(),
        name="insert_slices",
    )(every, expo, images, weight, trig, sums, kernels, codes)


def reduce_kernel(
    part, out_ref, cores, x_out, x_in, x_own, z_out, z_in, z_own, y_out, y_in, send, recv
):
    x, zh, c, ori = place()
    y, zl = ori // 2, ori % 2
    z = zh * 2 + zl

    def dev(xx, zz, cc, yy):
        return (xx * 8 + (zz // 2) * 2 + cc, yy * 2 + zz % 2)

    core_peer = dev(x, z, 1 - c, y)
    x_peers = [dev(lax.rem(x + s, 4), z, c, y) for s in range(1, 4)]
    z_peers = [dev(x, lax.rem(z + s, 8), c, y) for s in range(1, 8)]
    y_peers = [dev(x, z, c, lax.rem(y + s, 8)) for s in range(1, 8)]
    barrier = pltpu.get_barrier_semaphore()
    for peer in [core_peer] + x_peers + z_peers + y_peers:
        pl.semaphore_signal(barrier, inc=1, device_id=peer, device_id_type=MESH)
    pl.semaphore_wait(barrier, 18)

    def put(src, dst, sem, peer):
        copy = pltpu.make_async_remote_copy(
            src_ref=src, dst_ref=dst, send_sem=send.at[sem], recv_sem=recv.at[sem],
            device_id=peer, device_id_type=MESH,
        )
        copy.start()
        return copy

    def half(cc):
        return pl.ds(pl.multiple_of(cc * 256, 256), 256)

    sent = [put(part.at[:, half(1 - c)], cores, 0, core_peer)]
    sent[0].wait_recv()
    for k in range(3):
        total = part[k, half(c), :] + cores[k]
        x_out[:, k * 256 : k * 256 + 256] = total.astype(BF16)
        cores[k] = total

    def chunk(xx):
        return pl.ds(pl.multiple_of(xx * 64, 64), 64)

    steps = [
        put(x_out.at[chunk(lax.rem(x + s, 4))], x_in.at[s - 1], s, x_peers[s - 1])
        for s in range(1, 4)
    ]
    for copy in steps:
        copy.wait_recv()
    sent += steps
    for k in range(3):
        lanes = slice(k * 256, k * 256 + 256)
        total = cores[k, chunk(x), :]
        for s in range(3):
            total = total + x_in[s, :, lanes].astype(F32)
        x_own[:, lanes] = total
    for zz in range(8):
        rows = x_own[zz * 8 : zz * 8 + 8, :]
        rows = jnp.concatenate([rows[:, :384], rows[:, 384:]], axis=0)
        z_own[zz] = rows
        z_out[zz] = rows.astype(BF16)
    steps = [
        put(z_out.at[lax.rem(z + s, 8)], z_in.at[s - 1], 3 + s, z_peers[s - 1])
        for s in range(1, 8)
    ]
    for copy in steps:
        copy.wait_recv()
    sent += steps
    total = z_own[z]
    for s in range(7):
        total = total + z_in[s].astype(F32)
    for yy in range(8):
        for j in range(6):
            row = (j // 3) * 8 + yy
            y_out[yy, j : j + 1, :] = total[row : row + 1, (j % 3) * 128 : (j % 3) * 128 + 128]
        y_out[yy, 6:8, :] = jnp.zeros((2, 128), F32)
    steps = [
        put(y_out.at[lax.rem(y + s, 8)], y_in.at[s - 1], 10 + s, y_peers[s - 1])
        for s in range(1, 8)
    ]
    for copy in steps:
        copy.wait_recv()
    sent += steps
    total = y_out[y]
    for s in range(7):
        total = total + y_in[s]
    out_ref[...] = total
    for copy in sent:
        copy.wait_send()


def reduce(part):
    return pl.pallas_call(
        reduce_kernel,
        out_shape=jax.ShapeDtypeStruct((8, 128), F32),
        in_specs=vmem(1),
        out_specs=pl.BlockSpec(memory_space=pltpu.VMEM),
        scratch_shapes=[
            pltpu.VMEM((3, 256, 256), F32),
            pltpu.VMEM((256, 768), BF16),
            pltpu.VMEM((3, 64, 768), BF16),
            pltpu.VMEM((64, 768), F32),
            pltpu.VMEM((8, 16, 384), BF16),
            pltpu.VMEM((7, 16, 384), BF16),
            pltpu.VMEM((8, 16, 384), F32),
            pltpu.VMEM((8, 8, 128), F32),
            pltpu.VMEM((7, 8, 128), F32),
            pltpu.SemaphoreType.DMA((18,)),
            pltpu.SemaphoreType.DMA((18,)),
        ],
        compiler_params=params(collective_id=2, has_side_effects=True),
        name="reduce_volume",
    )(part)


def fold(raw):
    return pl.pallas_call(
        fold_kernel,
        out_shape=(
            jax.ShapeDtypeStruct((FREQ, 16, 256), BF16),
            jax.ShapeDtypeStruct((2, FREQ, 256), BF16),
        ),
        in_specs=vmem(1),
        out_specs=vmem(2),
        scratch_shapes=[pltpu.VMEM((2, FREQ, 256), F32)],
        compiler_params=params(),
        name="fold_rows",
    )(raw)


def weight_rows(noise_weight):
    grid = noise_weight.reshape(128, 64)
    up = grid[64:]
    down = jnp.concatenate([jnp.zeros((1, 64), F32), grid[63:0:-1]], axis=0)
    body = jnp.concatenate([up, down], axis=1)
    last = jnp.concatenate([jnp.zeros((64,), F32), grid[0]])[None]
    return jnp.concatenate([body, last, jnp.zeros((7, 128), F32)], axis=0)


def cell_counts(shifts):
    size = jnp.arange(4)
    side = jnp.array([1, -1])
    shift_y = jnp.arange(-3, 4)
    col = side[:, None] * size[None, :]
    live = (side[:, None] > 0) | (size[None, :] > 0)
    hit = (
        (shifts[:, 0][:, None, None, None] == col[None, :, None, :])
        & (shifts[:, 1][:, None, None, None] == shift_y[None, None, :, None])
        & live[None, :, None, :]
    )
    count = jnp.sum(hit.astype(F32), axis=0).reshape(14, 4)
    count = jnp.broadcast_to(count[:, :, None], (14, 4, IMGS)).reshape(14, 128)
    return jnp.concatenate([count, jnp.zeros((2, 128), F32)], axis=0)


def target_codes(targets, core):
    own = lax.dynamic_index_in_dim(targets.reshape(16, 2, 2, 64), core, 1, keepdims=False)
    own = own.reshape(ORI, 64).T
    owner, k = own // 3, own % 3
    core_at = (owner // 16) % 2
    z_hi = (owner // 32) % 4
    x = owner // 128
    y = (owner // 2) % 8
    z = z_hi * 2 + owner % 2
    row = ((core_at * 4 + x) * 8 + z) * 8 + y
    return (k * 512 + row).reshape(16, 128)


def shards(images, slices, noise_weight, shifts, kernels, targets):
    core = lax.axis_index("dom") % 2
    trig, sums = (jnp.asarray(t) for t in tables())
    raw = jnp.concatenate([images.reshape(16, 2 * PIX), slices.reshape(2, 2 * PIX)], axis=0)
    weight = weight_rows(noise_weight)
    counts = cell_counts(shifts)
    codes = target_codes(targets, core)
    own_images, own_slices = fold(raw)
    all_images, all_slices = gather(own_images, own_slices)
    all_slices = all_slices.reshape(ORI, FREQ, 256)
    expo, stats = scores(all_slices, all_images, weight, trig, sums, counts)
    every = exchange(stats)
    part, loglik = insert(every, expo, all_images, weight, trig, sums, kernels, codes)
    volume = reduce(part)
    loglik = lax.dynamic_slice_in_dim(loglik[0], core * 16, 16)
    return volume[:6].reshape(3, 2, 128), loglik


def solution(mesh):
    placed = (
        P("dom", None, None),
        P(("orient", "dom"), None, None),
        P(),
        P(),
        P(),
        P("orient", None),
    )
    return jax.shard_map(
        shards,
        mesh=mesh,
        in_specs=placed,
        out_specs=(P(("dom", "orient"), None, None), P("dom")),
        check_vma=False,
    )
```

```python
import jax
import jax.numpy as jnp
import numpy as np
from jax import lax
from jax.experimental import pallas as pl
from jax.experimental.pallas import tpu as pltpu
from jax.sharding import PartitionSpec as P

F32 = jnp.float32
BF16 = jnp.bfloat16
MESH = pl.DeviceIdType.MESH
PIX = 8192
TRANS = 49
FREQ = 64
IMGS = 32
ORI = 32
STEPS = FREQ + 1
VMEM_LIMIT = 56 * 1024 * 1024


def tables():
    kx = np.arange(64)
    unit = 2.0 * np.pi / 128.0
    rows = np.zeros((8, 128), np.float32)
    for a in range(4):
        rows[a, :64] = rows[a, 64:] = np.cos(unit * a * kx)
    for a in range(1, 4):
        rows[4 + a, :64] = np.sin(unit * a * kx)
        rows[4 + a, 64:] = -np.sin(unit * a * kx)
    m = np.arange(STEPS)
    sums = np.zeros((STEPS, 8, 128), np.float32)
    for b in range(4):
        sums[:, b, :] = np.cos(unit * b * m)[:, None]
        sums[:, 4 + b, :] = np.where(m == 64, 0.0, np.sin(unit * b * m))[:, None]
    return rows, sums


def entry_of(sigma, shift_y):
    return (0 if sigma > 0 else 7) + shift_y + 3


def fold_pair(m, block, low):
    if m % 2 == 0:
        first = block(32 + m // 2)
        second = pltpu.roll(block(32 - m // 2 if m else 0), 64, 1)
    else:
        first = pltpu.roll(block(32 + (m - 1) // 2), 64, 1)
        second = block(32 - (m + 1) // 2)
    return jnp.where(low, first, second)


def aligned_rows(pair, factors):
    real, imag = pair[:, :128], pair[:, 128:]
    rows = []
    for r in range(8):
        row = factors[r : r + 1]
        if r == 4:
            rows.append(jnp.zeros((IMGS, 256), F32))
        else:
            rows.append(jnp.concatenate([real * row, imag * row], axis=1))
    return rows


def merge_stats(stats):
    peak = stats[0][0:1]
    for part in stats[1:]:
        peak = jnp.maximum(peak, part[0:1])
    mass = jnp.zeros_like(peak)
    for part in stats:
        mass = mass + part[1:2] * jnp.exp(part[0:1] - peak)
    return peak, mass


def step_kernel(
    images_hbm, slices_hbm, noise_weight, shifts, kernels_hbm, targets, trig, sums,
    volume_ref, loglik_ref,
    images_raw, slices_raw, kernels,
    fold_rows, image_real, image_imag, images, slices, weight, high, low_part, real, imag, energy, acc, expo,
    counts, codes, chosen, post, back, folded, inserted, part, cores,
    stats_own, stats_near, stats_mid, stats_far,
    x_out, x_in, x_own, z_out, z_in, z_own, y_out, y_in,
    send, recv, local,
):
    dom, ori = lax.axis_index("dom"), lax.axis_index("orient")
    c, zh, x = dom % 2, (dom // 2) % 4, dom // 8
    y, zl = ori // 2, ori % 2
    z = zh * 2 + zl

    def dev(dx, dz, dc, dy):
        xx, zz, yy = lax.rem(x + dx, 4), lax.rem(z + dz, 8), lax.rem(y + dy, 8)
        cc = 1 - c if dc else c
        return (xx * 8 + (zz // 2) * 2 + cc, yy * 2 + zz % 2)

    def dev_zl(dl, dc):
        cc = 1 - c if dc else c
        ll = 1 - zl if dl else zl
        return (x * 8 + zh * 2 + cc, y * 2 + ll)

    core_peer = dev(0, 0, 1, 0)
    x_peers = [dev(s, 0, 0, 0) for s in range(1, 4)]
    z_peers = [dev(0, s, 0, 0) for s in range(1, 8)]
    y_peers = [dev(0, 0, 0, s) for s in range(1, 8)]
    near_peers = [core_peer, dev_zl(1, 0), dev_zl(1, 1)]
    barrier = pltpu.get_barrier_semaphore()
    everyone = [core_peer, near_peers[2]] + x_peers + z_peers + y_peers
    for peer in everyone:
        pl.semaphore_signal(barrier, inc=1, device_id=peer, device_id_type=MESH)

    get_slices = pltpu.make_async_copy(slices_hbm, slices_raw, local.at[0])
    get_slices.start()
    get_images = pltpu.make_async_copy(images_hbm, images_raw, local.at[1])
    get_images.start()
    get_kernels = pltpu.make_async_copy(kernels_hbm, kernels, local.at[2])
    get_kernels.start()

    sends = []

    def put(src, dst, sem, peer):
        copy = pltpu.make_async_remote_copy(
            src_ref=src, dst_ref=dst, send_sem=send.at[sem], recv_sem=recv.at[sem],
            device_id=peer, device_id_type=MESH,
        )
        copy.start()
        sends.append(copy)
        return copy

    def got(ref, sem):
        pltpu.make_async_remote_copy(
            src_ref=ref, dst_ref=ref, send_sem=send.at[sem], recv_sem=recv.at[sem],
            device_id=core_peer, device_id_type=MESH,
        ).wait_recv()

    low = lax.broadcasted_iota(jnp.int32, (1, 128), 1) < 64
    sign = jnp.where(low, 1.0, -1.0).astype(F32)

    home = x * 4 + zh
    get_slices.wait()
    for j in range(2):
        for m in range(FREQ):
            both = fold_pair(
                m, lambda b: slices_raw[j, :, b * 128 : b * 128 + 128].astype(F32), low
            )
            fold_rows[m : m + 1, :128] = both[0:1]
            fold_rows[m : m + 1, 128:] = both[1:2]
        slices[home, j] = fold_rows[...].astype(BF16)

    def fold_images(first, count):
        def one(i, carry):
            for m in range(FREQ):
                both = fold_pair(
                    m, lambda b: images_raw[i, :, b * 128 : b * 128 + 128].astype(F32), low
                )
                row = pl.ds(m * 16 + i, 1)
                image_real[row, :] = both[0:1]
                image_imag[row, :] = both[1:2]
            return carry

        lax.fori_loop(first, first + count, one, 0)

    def image_half(cc):
        return pl.ds(pl.multiple_of(cc * 16, 16), 16)

    def send_images():
        def one(m, carry):
            at = pl.ds(pl.multiple_of(m * 16, 16), 16)
            rows = jnp.concatenate([image_real[at, :], image_imag[at, :]], axis=1)
            images[m, image_half(c), :] = rows.astype(BF16)
            return carry

        lax.fori_loop(0, FREQ, one, 0)
        here = images.at[:, image_half(c)]
        put(here, here, 0, core_peer)

    def fold_weight():
        for m in range(FREQ):
            row = fold_pair(m, lambda b: noise_weight[b : b + 1, :], low)
            if m == 0:
                weight[FREQ : FREQ + 1, :] = jnp.where(low, 0.0, row)
                row = jnp.where(low, row, 0.0)
            weight[m : m + 1, :] = row

    def count_cells():
        row = lax.broadcasted_iota(jnp.int32, (16, 128), 0)
        size = lax.broadcasted_iota(jnp.int32, (16, 128), 1) // IMGS
        total = jnp.zeros((16, 128), F32)
        for t in range(TRANS):
            shift_x, shift_y = shifts[t, 0], shifts[t, 1]
            at = jnp.where(shift_x >= 0, 3, 10) + shift_y
            hit = (row == at) & (size == jnp.abs(shift_x))
            total = total + jnp.where(hit, 1.0, 0.0)
        counts[...] = total

    def find_codes():
        block = targets[...]
        owner = (block * 43691) >> 17
        k = block - 3 * owner
        core_at, z_hi_at, x_at = (owner >> 4) & 1, (owner >> 5) & 3, owner >> 7
        y_at, z_lo_at = (owner >> 1) & 7, owner & 1
        code = (core_at * 4 + x_at) * 192 + k * 64 + (z_hi_at * 2 + z_lo_at) * 8 + y_at
        orient = lax.broadcasted_iota(jnp.int32, (64, ORI), 0)
        mine = lax.broadcasted_iota(jnp.int32, (64, ORI), 1)
        pick = orient == (mine // 2) * 4 + c * 2 + mine % 2
        pick = jnp.where(pick, 1.0, 0.0).astype(BF16)
        dims = (((0,), (0,)), ((), ()))
        upper, lower = (code >> 5).astype(F32), (code & 31).astype(F32)
        upper = lax.dot_general(upper.astype(BF16), pick, dims, preferred_element_type=F32)
        lower = lax.dot_general(lower.astype(BF16), pick, dims, preferred_element_type=F32)
        code = upper * 32.0 + lower
        codes[...] = jnp.concatenate([code[16 * q : 16 * q + 16] for q in range(4)], axis=1)

    def choose(first, count):
        def one(t, carry):
            rows = lax.broadcasted_iota(jnp.int32, (128, 128), 0).astype(F32)
            rows = rows + (t * 128).astype(F32)
            at = pl.ds(pl.multiple_of(t * 128, 128), 128)
            for j in range(16):
                hit = rows == codes[j : j + 1, :]
                chosen[at, j * 128 : j * 128 + 128] = jnp.where(hit, 1.0, 0.0).astype(BF16)
            return carry

        lax.fori_loop(first, first + count, one, 0)

    def wait_images():
        got(images.at[:, image_half(1 - c)], 0)

    def align(first, count):
        def one(m, carry):
            factors = trig[...] * weight[pl.ds(m, 1), :]
            rows = aligned_rows(images[lax.rem(m, FREQ)].astype(F32), factors)
            for r, row in enumerate(rows):
                top = row.astype(BF16)
                high[m, r * IMGS : (r + 1) * IMGS, :] = top
                low_part[m, r * IMGS : (r + 1) * IMGS, :] = (row - top.astype(F32)).astype(BF16)
            return carry

        lax.fori_loop(first, first + count, one, 0)

    def slot(dx, dz):
        return lax.rem(x + dx, 4) * 4 + lax.rem(zh + dz, 4)

    def piece(dx, dz, h):
        return slices.at[slot(dx, dz), :, pl.ds(h * 32, 32)]

    def single(dx, dz, h, j):
        return slices.at[slot(dx, dz), j, pl.ds(h * 32, 32)]

    def gsem(kind, h):
        return 1 + kind * 2 + h

    z_up, z_down, x_up, x_down = z_peers[1], z_peers[5], x_peers[0], x_peers[2]

    def along_z(h):
        here = piece(0, 0, h)
        put(here, here, gsem(0, h), z_up)
        put(here, here, gsem(1, h), z_down)

    def along_x(dz, h):
        here = piece(0, dz, h)
        put(here, here, gsem(4 + 4 * dz, h), x_up)
        put(here, here, gsem(5 + 4 * dz, h), x_down)

    def pass_z(h):
        got(piece(0, 3, h), gsem(0, h))
        half = single(0, 3, h, 0)
        put(half, half, gsem(2, h), z_up)
        along_x(3, h)
        got(piece(0, 1, h), gsem(1, h))
        half = single(0, 1, h, 1)
        put(half, half, gsem(3, h), z_down)
        along_x(1, h)

    def far_z(h):
        got(single(0, 2, h, 0), gsem(2, h))
        got(single(0, 2, h, 1), gsem(3, h))
        along_x(2, h)

    def pass_x(dz, h):
        got(piece(3, dz, h), gsem(4 + 4 * dz, h))
        half = single(3, dz, h, 0)
        put(half, half, gsem(6 + 4 * dz, h), x_up)
        got(piece(1, dz, h), gsem(5 + 4 * dz, h))
        half = single(1, dz, h, 1)
        put(half, half, gsem(7 + 4 * dz, h), x_down)

    def far_x(dz, h):
        got(single(2, dz, h, 0), gsem(6 + 4 * dz, h))
        got(single(2, dz, h, 1), gsem(7 + 4 * dz, h))

    get_images.wait()
    fold_images(0, 4)
    pl.semaphore_wait(barrier, len(everyone))
    for h in range(2):
        along_z(h)
        along_x(0, h)
    fold_images(4, 6)
    pass_x(0, 0)
    pass_x(0, 1)
    pass_z(0)
    pass_z(1)
    fold_images(10, 6)
    send_images()
    pass_x(3, 0)
    pass_x(1, 0)
    far_z(0)
    fold_weight()
    pass_x(3, 1)
    pass_x(1, 1)
    far_z(1)
    wait_images()
    align(0, 20)
    pass_x(2, 0)
    pass_x(2, 1)
    align(20, 45)
    count_cells()
    find_codes()
    choose(0, 12)

    acc[...] = jnp.zeros_like(acc)
    energy[...] = jnp.zeros_like(energy)

    def widen(h):
        def one(o, carry):
            block = slices[o // 2, lax.rem(o, 2), pl.ds(h * 32, 32), :].astype(F32)
            rows = pl.ds(pl.multiple_of(o * FREQ + h * 32, 32), 32)
            real[rows, :] = block[:, :128]
            imag[rows, :] = block[:, 128:]
            return carry

        lax.fori_loop(0, ORI, one, 0)

    def correlate(m, src):
        at = pl.ds(src, ORI, stride=FREQ)
        s_r, s_i = real[at, :], imag[at, :]
        energy[...] += weight[pl.ds(m, 1), :] * (s_r * s_r + s_i * s_i)
        left = jnp.concatenate(
            [
                jnp.concatenate([s_r, s_i], axis=1),
                jnp.concatenate([-sign * s_i, sign * s_r], axis=1),
            ],
            axis=0,
        ).astype(BF16)
        dims = (((1,), (1,)), ((), ()))
        return lax.dot_general(
            left, high[m], dims, preferred_element_type=F32
        ) + lax.dot_general(left, low_part[m], dims, preferred_element_type=F32)

    def add_scores(parts):
        for b in range(4):
            for k in range(2):
                for half in range(2):
                    even = k == half
                    if b == 0 and not even:
                        continue
                    lanes = slice(half * 128, half * 128 + 128)
                    total = acc[b, k * ORI : (k + 1) * ORI, lanes]
                    for m, value in parts:
                        value = value[k * ORI : (k + 1) * ORI, lanes]
                        if b:
                            value = value * sums[m, pl.ds(b if even else 4 + b, 1), :]
                        total = total + value
                    acc[b, k * ORI : (k + 1) * ORI, lanes] = total

    def score_half(h):
        widen(h)

        def some(group, carry):
            steps = [h * 32 + group * 4 + j for j in range(4)]
            add_scores([(m, correlate(m, m)) for m in steps])
            return carry

        lax.fori_loop(0, 8, some, 0)

    for dz in range(4):
        far_x(dz, 0)
    score_half(0)
    add_scores([(FREQ, correlate(FREQ, 0))])
    for dz in range(4):
        far_x(dz, 1)
    score_half(1)

    half_energy = 0.5 * jnp.sum(energy[...], axis=1, keepdims=True)
    peak = jnp.full((ORI, 128), -1e30, F32)
    for b in range(4):
        q1 = acc[b, :ORI, :128] - half_energy
        q2 = acc[b, :ORI, 128:]
        q4 = acc[b, ORI:, :128]
        q3 = acc[b, ORI:, 128:]
        for tau in (1, -1) if b else (1,):
            for sigma in (1, -1):
                entry = entry_of(sigma, tau * b)
                value = q1 - sigma * q3
                if b:
                    value = value - tau * (sigma * q2 + q4)
                expo[entry] = value
                live = counts[entry : entry + 1, :] > 0
                peak = jnp.maximum(peak, jnp.where(live, value, -1e30))
    peak = jnp.max(peak, axis=0, keepdims=True)
    peak = jnp.maximum(peak, pltpu.roll(peak, 32, 1))
    peak = jnp.maximum(peak, pltpu.roll(peak, 64, 1))
    mass = jnp.zeros((ORI, 128), F32)
    for entry in range(14):
        count = counts[entry : entry + 1, :]
        value = jnp.where(count > 0, expo[entry] - peak, -1e30)
        value = jnp.exp(value) * count
        expo[entry] = value
        mass = mass + value
    mass = jnp.sum(mass, axis=0, keepdims=True)
    mass = mass + pltpu.roll(mass, 32, 1)
    mass = mass + pltpu.roll(mass, 64, 1)
    own_peak = peak
    rest = jnp.zeros((6, 128), F32)
    stats_own[...] = jnp.concatenate([peak, mass, rest], axis=0)

    near = [put(stats_own, stats_near.at[s], 41 + s, near_peers[s]) for s in range(3)]
    for b in range(4):
        q1 = jnp.zeros((ORI, 128), F32)
        q2, q3, q4 = q1, q1, q1
        for tau in (1, -1) if b else (1,):
            for sigma in (1, -1):
                value = expo[entry_of(sigma, tau * b)]
                q1 = q1 + value
                q2 = q2 - (sigma * tau) * value
                q3 = q3 - sigma * value
                q4 = q4 - tau * value
        post[b, :ORI, :128] = q1
        post[b, :ORI, 128:] = q2
        post[b, ORI:, :128] = q4
        post[b, ORI:, 128:] = q3

    def spread(first, count):
        def one(m, carry):
            for k in range(2):
                for half in range(2):
                    even = k == half
                    lanes = slice(half * 128, half * 128 + 128)
                    total = None
                    for b in range(4):
                        if b == 0 and not even:
                            continue
                        value = post[b, k * ORI : (k + 1) * ORI, lanes]
                        if b:
                            value = value * sums[m, pl.ds(b if even else 4 + b, 1), :]
                        total = value if total is None else total + value
                    back[m, k * ORI : (k + 1) * ORI, lanes] = total
            return carry

        lax.fori_loop(first, first + count, one, 0)

    for copy in near:
        copy.wait_recv()
    peak, mass = merge_stats([stats_own[...]] + [stats_near[s] for s in range(3)])
    stats_mid[...] = jnp.concatenate([peak, mass, rest], axis=0)
    far = [put(stats_mid, stats_far.at[s], 44 + s, y_peers[s]) for s in range(7)]
    spread(0, STEPS)
    for copy in far:
        copy.wait_recv()
    peak, mass = merge_stats([stats_mid[...]] + [stats_far[s] for s in range(7)])
    loglik = peak + jnp.log(mass)
    loglik_ref[...] = jnp.where(c == 0, loglik[:, :16], loglik[:, 16:32])
    scale = jnp.exp(own_peak - peak) / mass
    scale = jnp.concatenate([scale, scale], axis=1)

    def collect(m):
        grad = jnp.dot((back[m] * scale).astype(BF16), high[m], preferred_element_type=F32)
        out_real = grad[:ORI, :128] + sign * grad[ORI:, 128:]
        out_imag = grad[:ORI, 128:] - sign * grad[ORI:, :128]
        return jnp.concatenate([out_real, out_imag], axis=0)

    def some_back(group, carry):
        for j in range(4):
            m = group * 4 + j
            folded[m] = collect(m)
        return carry

    lax.fori_loop(0, FREQ // 4, some_back, 0)
    folded[0] = folded[0] + collect(FREQ)
    get_kernels.wait()

    def insert(block, first, second):
        value = jnp.where(low, first, second)
        top = value.astype(BF16)
        left = jnp.concatenate([top, (value - top.astype(F32)).astype(BF16)], axis=0)
        out = jnp.dot(left, kernels[block], preferred_element_type=F32)
        out = out[: 2 * ORI] + out[2 * ORI :]
        at = lax.rem(block, 16) * 128 + (block // 16) * ORI
        rows = pl.ds(pl.multiple_of(at, ORI), ORI)
        inserted[rows, :] = jnp.concatenate([out[:ORI], out[ORI:]], axis=1).astype(BF16)

    def some_insert(group, carry):
        for j in range(2):
            b = group * 2 + j
            insert(32 + b, folded[2 * b], pltpu.roll(folded[2 * b + 1], 64, 1))
            m = FREQ - 2 * b
            insert(b, pltpu.roll(folded[lax.rem(m, FREQ)], 64, 1), folded[m - 1])
        return carry

    lax.fori_loop(0, 16, some_insert, 0)

    def scatter(cc):
        def one(t, carry):
            rows = pl.ds(pl.multiple_of(cc * 768 + t * 256, 256), 256)
            part[rows, :] = jnp.dot(
                chosen[rows, :], inserted[...], preferred_element_type=F32
            )
            return carry

        lax.fori_loop(0, 3, one, 0)

    def core_rows(cc):
        return pl.ds(pl.multiple_of(cc * 768, 768), 768)

    scatter(1 - c)
    to_core = put(part.at[core_rows(1 - c)], cores, 51, core_peer)
    scatter(c)
    to_core.wait_recv()

    def chunk(xx):
        return pl.ds(pl.multiple_of(xx * 192, 192), 192)

    def own_chunk(xx):
        return pl.ds(pl.multiple_of(c * 768 + xx * 192, 192), 192)

    steps = []
    for s in (2, 1, 3):
        xx = lax.rem(x + s, 4)
        x_out[s - 1] = (part[own_chunk(xx), :] + cores[chunk(xx), :]).astype(BF16)
        steps.append(put(x_out.at[s - 1], x_in.at[s - 1], 51 + s, x_peers[s - 1]))
    x_own[...] = part[own_chunk(x), :] + cores[chunk(x), :]
    for copy in steps:
        copy.wait_recv()
    x_own[...] += sum(x_in[s].astype(F32) for s in range(3))
    for zz in range(8):
        rows = jnp.concatenate(
            [x_own[k * 64 + zz * 8 : k * 64 + zz * 8 + 8, :] for k in range(3)], axis=1
        )
        rows = jnp.concatenate([rows[:, :384], rows[:, 384:]], axis=0)
        z_own[zz] = rows
        z_out[zz] = rows.astype(BF16)
    steps = [
        put(z_out.at[lax.rem(z + s, 8)], z_in.at[s - 1], 54 + s, z_peers[s - 1])
        for s in range(1, 8)
    ]
    for copy in steps:
        copy.wait_recv()
    total = z_own[z]
    for s in range(7):
        total = total + z_in[s].astype(F32)
    for yy in range(8):
        for j in range(6):
            row = (j // 3) * 8 + yy
            y_out[yy, j : j + 1, :] = total[row : row + 1, (j % 3) * 128 : (j % 3) * 128 + 128]
        y_out[yy, 6:8, :] = jnp.zeros((2, 128), F32)
    steps = [
        put(y_out.at[lax.rem(y + s, 8)], y_in.at[s - 1], 61 + s, y_peers[s - 1])
        for s in range(1, 8)
    ]
    for copy in steps:
        copy.wait_recv()
    total = y_out[y]
    for s in range(7):
        total = total + y_in[s]
    for k in range(3):
        volume_ref[k] = total[2 * k : 2 * k + 2]
    for copy in sends:
        copy.wait_send()


def shards(images, slices, noise_weight, shifts, kernels, targets):
    trig, sums = tables()
    in_vmem = pl.BlockSpec(memory_space=pltpu.VMEM)
    in_smem = pl.BlockSpec(memory_space=pltpu.SMEM)
    anywhere = pl.BlockSpec(memory_space=pl.ANY)
    volume, loglik = pl.pallas_call(
        step_kernel,
        out_shape=(
            jax.ShapeDtypeStruct((3, 2, 128), F32),
            jax.ShapeDtypeStruct((1, 16), F32),
        ),
        in_specs=[
            anywhere, anywhere, in_vmem, in_smem, anywhere, in_vmem, in_vmem, in_vmem,
        ],
        out_specs=(in_vmem, in_vmem),
        scratch_shapes=[
            pltpu.VMEM((16, 2, PIX), BF16),
            pltpu.VMEM((2, 2, PIX), BF16),
            pltpu.VMEM((64, 128, 128), BF16),
            pltpu.VMEM((FREQ, 256), F32),
            pltpu.VMEM((FREQ * 16, 128), F32),
            pltpu.VMEM((FREQ * 16, 128), F32),
            pltpu.VMEM((FREQ, IMGS, 256), BF16),
            pltpu.VMEM((16, 2, FREQ, 256), BF16),
            pltpu.VMEM((72, 128), F32),
            pltpu.VMEM((STEPS, 256, 256), BF16),
            pltpu.VMEM((STEPS, 256, 256), BF16),
            pltpu.VMEM((ORI * FREQ, 128), F32),
            pltpu.VMEM((ORI * FREQ, 128), F32),
            pltpu.VMEM((ORI, 128), F32),
            pltpu.VMEM((4, 2 * ORI, 256), F32),
            pltpu.VMEM((14, ORI, 128), F32),
            pltpu.VMEM((16, 128), F32),
            pltpu.VMEM((16, 128), F32),
            pltpu.VMEM((1536, 2048), BF16),
            pltpu.VMEM((4, 2 * ORI, 256), F32),
            pltpu.VMEM((STEPS, 2 * ORI, 256), F32),
            pltpu.VMEM((FREQ, 2 * ORI, 128), F32),
            pltpu.VMEM((FREQ * ORI, 256), BF16),
            pltpu.VMEM((1536, 256), F32),
            pltpu.VMEM((768, 256), F32),
            pltpu.VMEM((8, 128), F32),
            pltpu.VMEM((3, 8, 128), F32),
            pltpu.VMEM((8, 128), F32),
            pltpu.VMEM((7, 8, 128), F32),
            pltpu.VMEM((3, 192, 256), BF16),
            pltpu.VMEM((3, 192, 256), BF16),
            pltpu.VMEM((192, 256), F32),
            pltpu.VMEM((8, 16, 384), BF16),
            pltpu.VMEM((7, 16, 384), BF16),
            pltpu.VMEM((8, 16, 384), F32),
            pltpu.VMEM((8, 8, 128), F32),
            pltpu.VMEM((7, 8, 128), F32),
            pltpu.SemaphoreType.DMA((69,)),
            pltpu.SemaphoreType.DMA((69,)),
            pltpu.SemaphoreType.DMA((3,)),
        ],
        compiler_params=pltpu.CompilerParams(
            vmem_limit_bytes=VMEM_LIMIT, collective_id=0, has_side_effects=True
        ),
        name="expectation_step",
    )(
        images, slices, noise_weight.reshape(64, 128), shifts, kernels, targets,
        jnp.asarray(trig), jnp.asarray(sums),
    )
    return volume, loglik.reshape(16)


def solution(mesh):
    placed = (
        P("dom", None, None),
        P(("orient", "dom"), None, None),
        P(),
        P(),
        P(),
        P("orient", None),
    )
    return jax.shard_map(
        shards,
        mesh=mesh,
        in_specs=placed,
        out_specs=(P(("dom", "orient"), None, None), P("dom")),
        check_vma=False,
    )
```

```python
import jax
import jax.numpy as jnp
import numpy as np
from jax import lax
from jax.experimental import pallas as pl
from jax.experimental.pallas import tpu as pltpu
from jax.sharding import PartitionSpec as P

F32 = jnp.float32
BF16 = jnp.bfloat16
MESH = pl.DeviceIdType.MESH
PIX = 8192
TRANS = 49
FREQ = 64
IMGS = 32
ORI = 32
STEPS = FREQ + 1
VMEM_LIMIT = 56 * 1024 * 1024


def tables():
    kx = np.arange(64)
    unit = 2.0 * np.pi / 128.0
    rows = np.zeros((8, 128), np.float32)
    for a in range(4):
        rows[a, :64] = rows[a, 64:] = np.cos(unit * a * kx)
    for a in range(1, 4):
        rows[4 + a, :64] = np.sin(unit * a * kx)
        rows[4 + a, 64:] = -np.sin(unit * a * kx)
    m = np.arange(STEPS)
    sums = np.zeros((STEPS, 8, 128), np.float32)
    for b in range(4):
        sums[:, b, :] = np.cos(unit * b * m)[:, None]
        sums[:, 4 + b, :] = np.where(m == 64, 0.0, np.sin(unit * b * m))[:, None]
    return rows, sums


def entry_of(sigma, shift_y):
    return (0 if sigma > 0 else 7) + shift_y + 3


def fold_pair(m, block, low):
    if m % 2 == 0:
        first = block(32 + m // 2)
        second = pltpu.roll(block(32 - m // 2 if m else 0), 64, 1)
    else:
        first = pltpu.roll(block(32 + (m - 1) // 2), 64, 1)
        second = block(32 - (m + 1) // 2)
    return jnp.where(low, first, second)


def aligned_rows(pair, factors):
    real, imag = pair[:, :128], pair[:, 128:]
    rows = []
    for r in range(8):
        row = factors[r : r + 1]
        if r == 4:
            rows.append(jnp.zeros((IMGS, 256), F32))
        else:
            rows.append(jnp.concatenate([real * row, imag * row], axis=1))
    return rows


def merge_stats(stats):
    peak = stats[0][0:1]
    for part in stats[1:]:
        peak = jnp.maximum(peak, part[0:1])
    mass = jnp.zeros_like(peak)
    for part in stats:
        mass = mass + part[1:2] * jnp.exp(part[0:1] - peak)
    return peak, mass


def step_kernel(
    images_hbm, slices_hbm, noise_weight, shifts, kernels_hbm, targets, trig, sums_hbm, trig_t_hbm,
    volume_ref, loglik_ref,
    images_raw, slices_raw, kernels, sums,
    fold_rows, image_real, image_imag, images, slices, weight, trig_t, high, high_t, low_t, real, imag, energy, acc, expo,
    counts, codes, chosen, post, back, folded, inserted, part, cores,
    stats_own, stats_near, stats_mid, stats_far,
    x_out, x_in, x_own, z_out, z_in, z_own, y_out, y_in,
    send, recv, local,
):
    dom, ori = lax.axis_index("dom"), lax.axis_index("orient")
    c, zh, x = dom % 2, (dom // 2) % 4, dom // 8
    y, zl = ori // 2, ori % 2
    z = zh * 2 + zl

    def dev(dx, dz, dc, dy):
        xx, zz, yy = lax.rem(x + dx, 4), lax.rem(z + dz, 8), lax.rem(y + dy, 8)
        cc = 1 - c if dc else c
        return (xx * 8 + (zz // 2) * 2 + cc, yy * 2 + zz % 2)

    def dev_zl(dl, dc):
        cc = 1 - c if dc else c
        ll = 1 - zl if dl else zl
        return (x * 8 + zh * 2 + cc, y * 2 + ll)

    core_peer = dev(0, 0, 1, 0)
    x_peers = [dev(s, 0, 0, 0) for s in range(1, 4)]
    z_peers = [dev(0, s, 0, 0) for s in range(1, 8)]
    y_peers = [dev(0, 0, 0, s) for s in range(1, 8)]
    near_peers = [core_peer, dev_zl(1, 0), dev_zl(1, 1)]
    barrier = pltpu.get_barrier_semaphore()
    everyone = [core_peer, near_peers[2]] + x_peers + z_peers + y_peers
    for peer in everyone:
        pl.semaphore_signal(barrier, inc=1, device_id=peer, device_id_type=MESH)

    get_slices = pltpu.make_async_copy(slices_hbm, slices_raw, local.at[0])
    get_slices.start()
    get_images = pltpu.make_async_copy(images_hbm, images_raw, local.at[1])
    get_images.start()
    get_kernels = pltpu.make_async_copy(kernels_hbm, kernels, local.at[2])
    get_kernels.start()
    get_sums = pltpu.make_async_copy(sums_hbm, sums, local.at[3])
    get_sums.start()
    get_trig_t = pltpu.make_async_copy(trig_t_hbm, trig_t, local.at[4])
    get_trig_t.start()

    sends = []

    def put(src, dst, sem, peer):
        copy = pltpu.make_async_remote_copy(
            src_ref=src, dst_ref=dst, send_sem=send.at[sem], recv_sem=recv.at[sem],
            device_id=peer, device_id_type=MESH,
        )
        copy.start()
        sends.append(copy)
        return copy

    def got(ref, sem):
        pltpu.make_async_remote_copy(
            src_ref=ref, dst_ref=ref, send_sem=send.at[sem], recv_sem=recv.at[sem],
            device_id=core_peer, device_id_type=MESH,
        ).wait_recv()

    low = lax.broadcasted_iota(jnp.int32, (1, 128), 1) < 64
    sign = jnp.where(low, 1.0, -1.0).astype(F32)

    get_slices.wait()
    for j in range(2):
        for m in range(FREQ):
            both = fold_pair(
                m, lambda b: slices_raw[j, :, b * 128 : b * 128 + 128].astype(F32), low
            )
            fold_rows[m : m + 1, :128] = both[0:1]
            fold_rows[m : m + 1, 128:] = both[1:2]
        slices[0, j] = fold_rows[...].astype(BF16)

    def fold_images(first, count):
        def one(i, carry):
            for m in range(FREQ):
                both = fold_pair(
                    m, lambda b: images_raw[i, :, b * 128 : b * 128 + 128].astype(F32), low
                )
                row = pl.ds(m * 16 + i, 1)
                image_real[row, :] = both[0:1]
                image_imag[row, :] = both[1:2]
            return carry

        lax.fori_loop(first, first + count, one, 0)

    def image_half(cc):
        return pl.ds(pl.multiple_of(cc * 16, 16), 16)

    def send_images():
        def one(m, carry):
            at = pl.ds(pl.multiple_of(m * 16, 16), 16)
            rows = jnp.concatenate([image_real[at, :], image_imag[at, :]], axis=1)
            images[m, image_half(c), :] = rows.astype(BF16)
            return carry

        lax.fori_loop(0, FREQ, one, 0)
        here = images.at[:, image_half(c)]
        put(here, here, 0, core_peer)

    def fold_weight():
        for m in range(FREQ):
            row = fold_pair(m, lambda b: noise_weight[b : b + 1, :], low)
            if m == 0:
                weight[FREQ : FREQ + 1, :] = jnp.where(low, 0.0, row)
                row = jnp.where(low, row, 0.0)
            weight[m : m + 1, :] = row

    def count_cells():
        row = lax.broadcasted_iota(jnp.int32, (16, 128), 0)
        size = lax.broadcasted_iota(jnp.int32, (16, 128), 1) // IMGS
        total = jnp.zeros((16, 128), F32)
        for t in range(TRANS):
            shift_x, shift_y = shifts[0, t], shifts[1, t]
            at = jnp.where(shift_x >= 0, 3, 10) + shift_y
            hit = (row == at) & (size == jnp.abs(shift_x))
            total = total + jnp.where(hit, 1.0, 0.0)
        counts[...] = total

    def find_codes():
        block = targets[...]
        owner = (block * 43691) >> 17
        k = block - 3 * owner
        core_at, z_hi_at, x_at = (owner >> 4) & 1, (owner >> 5) & 3, owner >> 7
        y_at, z_lo_at = (owner >> 1) & 7, owner & 1
        code = (x_at * 2 + core_at) * 192 + k * 64 + (z_hi_at * 2 + z_lo_at) * 8 + y_at
        row = lax.broadcasted_iota(jnp.int32, (64, ORI), 0)
        mine = lax.broadcasted_iota(jnp.int32, (64, ORI), 1)
        x_from = (x + (mine >> 3)) & 3
        z_from = (zh + (mine >> 1)) & 3
        source = ((x_from * 4 + z_from) * 2 + c) * 2 + (mine & 1)
        pick = jnp.where(row == source, 1.0, 0.0).astype(BF16)
        dims = (((0,), (0,)), ((), ()))
        upper, lower = (code >> 5).astype(F32), (code & 31).astype(F32)
        upper = lax.dot_general(upper.astype(BF16), pick, dims, preferred_element_type=F32)
        lower = lax.dot_general(lower.astype(BF16), pick, dims, preferred_element_type=F32)
        code = upper * 32.0 + lower
        codes[...] = jnp.concatenate([code[16 * q : 16 * q + 16] for q in range(4)], axis=1)

    def choose(first, count):
        def one(t, carry):
            rows = lax.broadcasted_iota(jnp.int32, (128, 128), 0).astype(F32)
            rows = rows + (t * 128).astype(F32)
            at = pl.ds(pl.multiple_of(t * 128, 128), 128)
            for j in range(16):
                hit = rows == codes[j : j + 1, :]
                chosen[at, j * 128 : j * 128 + 128] = jnp.where(hit, 1.0, 0.0).astype(BF16)
            return carry

        lax.fori_loop(first, first + count, one, 0)

    def wait_images():
        got(images.at[:, image_half(1 - c)], 0)

    spread_images = jnp.where(
        lax.broadcasted_iota(jnp.int32, (2 * IMGS, 256), 0) % IMGS
        == lax.broadcasted_iota(jnp.int32, (2 * IMGS, 256), 1) % IMGS,
        1.0,
        0.0,
    ).astype(BF16)

    def align(first, count):
        def one(m, carry):
            factors = trig[...] * weight[pl.ds(m, 1), :]
            rows = aligned_rows(images[lax.rem(m, FREQ)].astype(F32), factors)
            for r, row in enumerate(rows):
                high[m, r * IMGS : (r + 1) * IMGS, :] = row.astype(BF16)
            return carry

        lax.fori_loop(first, first + count, one, 0)

    def align_turned(first, count):
        def one(m, carry):
            w = weight[pl.ds(m, 1), :]
            pair = images[lax.rem(m, FREQ)].astype(F32) * jnp.concatenate([w, w], axis=1)
            top = pair.astype(BF16)
            terms = jnp.concatenate([top, (pair - top.astype(F32)).astype(BF16)], axis=0)
            turned = lax.dot_general(
                terms, spread_images, (((0,), (0,)), ((), ())), preferred_element_type=F32
            )
            turned = turned * trig_t[...]
            top = turned.astype(BF16)
            high_t[m] = top
            low_t[m] = (turned - top.astype(F32)).astype(BF16)
            return carry

        lax.fori_loop(first, first + count, one, 0)

    def piece(dx, dz, h):
        return slices.at[dx * 4 + dz, :, pl.ds(h * 32, 32)]

    def single(dx, dz, h, j):
        return slices.at[dx * 4 + dz, j, pl.ds(h * 32, 32)]

    def gsem(kind, h):
        return 1 + kind * 2 + h

    z_up, z_down, x_up, x_down = z_peers[1], z_peers[5], x_peers[0], x_peers[2]

    def along_z(h):
        put(piece(0, 0, h), piece(0, 3, h), gsem(0, h), z_up)
        put(piece(0, 0, h), piece(0, 1, h), gsem(1, h), z_down)

    def along_x(dz, h):
        put(piece(0, dz, h), piece(3, dz, h), gsem(4 + 4 * dz, h), x_up)
        put(piece(0, dz, h), piece(1, dz, h), gsem(5 + 4 * dz, h), x_down)

    def pass_z(h):
        got(piece(0, 3, h), gsem(0, h))
        put(single(0, 3, h, 0), single(0, 2, h, 0), gsem(2, h), z_up)
        along_x(3, h)
        got(piece(0, 1, h), gsem(1, h))
        put(single(0, 1, h, 1), single(0, 2, h, 1), gsem(3, h), z_down)
        along_x(1, h)

    def far_z(h):
        got(single(0, 2, h, 0), gsem(2, h))
        got(single(0, 2, h, 1), gsem(3, h))
        along_x(2, h)

    def pass_x(dz, h):
        got(piece(3, dz, h), gsem(4 + 4 * dz, h))
        put(single(3, dz, h, 0), single(2, dz, h, 0), gsem(6 + 4 * dz, h), x_up)
        got(piece(1, dz, h), gsem(5 + 4 * dz, h))
        put(single(1, dz, h, 1), single(2, dz, h, 1), gsem(7 + 4 * dz, h), x_down)

    def far_x(dz, h):
        got(single(2, dz, h, 0), gsem(6 + 4 * dz, h))
        got(single(2, dz, h, 1), gsem(7 + 4 * dz, h))

    pl.semaphore_wait(barrier, len(everyone))
    for h in range(2):
        along_z(h)
        along_x(0, h)
    get_images.wait()
    fold_images(0, 16)
    send_images()
    fold_weight()
    count_cells()
    pass_z(0)
    pass_z(1)
    pass_x(0, 0)
    pass_x(0, 1)
    wait_images()
    get_trig_t.wait()
    align_turned(0, 24)
    far_z(0)
    far_z(1)
    for h in range(2):
        pass_x(3, h)
        pass_x(1, h)
    align_turned(24, 24)
    pass_x(2, 0)
    pass_x(2, 1)
    align_turned(48, 17)
    get_sums.wait()

    acc[...] = jnp.zeros_like(acc)
    energy[...] = jnp.zeros_like(energy)

    def widen(h):
        def one(o, carry):
            block = slices[o // 2, lax.rem(o, 2), pl.ds(h * 32, 32), :].astype(F32)
            rows = pl.ds(pl.multiple_of(o * FREQ + h * 32, 32), 32)
            real[rows, :] = block[:, :128]
            imag[rows, :] = block[:, 128:]
            return carry

        lax.fori_loop(0, ORI, one, 0)

    def correlate(m, src):
        at = pl.ds(src, ORI, stride=FREQ)
        s_r, s_i = real[at, :], imag[at, :]
        energy[...] += weight[pl.ds(m, 1), :] * (s_r * s_r + s_i * s_i)
        left = jnp.concatenate(
            [
                jnp.concatenate([s_r, s_i], axis=1),
                jnp.concatenate([-sign * s_i, sign * s_r], axis=1),
            ],
            axis=0,
        ).astype(BF16)
        return jnp.dot(left, high_t[m], preferred_element_type=F32) + jnp.dot(
            left, low_t[m], preferred_element_type=F32
        )

    def add_scores(parts):
        for b in range(4):
            for k in range(2):
                for half in range(2):
                    even = k == half
                    if b == 0 and not even:
                        continue
                    lanes = slice(half * 128, half * 128 + 128)
                    total = acc[b, k * ORI : (k + 1) * ORI, lanes]
                    for m, value in parts:
                        value = value[k * ORI : (k + 1) * ORI, lanes]
                        if b:
                            value = value * sums[m, pl.ds(b if even else 4 + b, 1), :]
                        total = total + value
                    acc[b, k * ORI : (k + 1) * ORI, lanes] = total

    def score_half(h):
        widen(h)

        def some(group, carry):
            steps = [h * 32 + group * 8 + j for j in range(8)]
            add_scores([(m, correlate(m, m)) for m in steps])
            return carry

        lax.fori_loop(0, 4, some, 0)

    for dz in range(4):
        far_x(dz, 0)
    score_half(0)
    add_scores([(FREQ, correlate(FREQ, 0))])
    for dz in range(4):
        far_x(dz, 1)
    score_half(1)

    half_energy = 0.5 * jnp.sum(energy[...], axis=1, keepdims=True)
    peak = jnp.full((ORI, 128), -1e30, F32)
    for b in range(4):
        q1 = acc[b, :ORI, :128] - half_energy
        q2 = acc[b, :ORI, 128:]
        q4 = acc[b, ORI:, :128]
        q3 = acc[b, ORI:, 128:]
        for tau in (1, -1) if b else (1,):
            for sigma in (1, -1):
                entry = entry_of(sigma, tau * b)
                value = q1 - sigma * q3
                if b:
                    value = value - tau * (sigma * q2 + q4)
                expo[entry] = value
                live = counts[entry : entry + 1, :] > 0
                peak = jnp.maximum(peak, jnp.where(live, value, -1e30))
    peak = jnp.max(peak, axis=0, keepdims=True)
    peak = jnp.maximum(peak, pltpu.roll(peak, 32, 1))
    peak = jnp.maximum(peak, pltpu.roll(peak, 64, 1))
    mass = jnp.zeros((ORI, 128), F32)
    for entry in range(14):
        count = counts[entry : entry + 1, :]
        value = jnp.where(count > 0, expo[entry] - peak, -1e30)
        value = jnp.exp(value) * count
        expo[entry] = value
        mass = mass + value
    mass = jnp.sum(mass, axis=0, keepdims=True)
    mass = mass + pltpu.roll(mass, 32, 1)
    mass = mass + pltpu.roll(mass, 64, 1)
    own_peak = peak
    rest = jnp.zeros((6, 128), F32)
    stats_own[...] = jnp.concatenate([peak, mass, rest], axis=0)

    near = [put(stats_own, stats_near.at[s], 41 + s, near_peers[s]) for s in range(3)]
    for b in range(4):
        q1 = jnp.zeros((ORI, 128), F32)
        q2, q3, q4 = q1, q1, q1
        for tau in (1, -1) if b else (1,):
            for sigma in (1, -1):
                value = expo[entry_of(sigma, tau * b)]
                q1 = q1 + value
                q2 = q2 - (sigma * tau) * value
                q3 = q3 - sigma * value
                q4 = q4 - tau * value
        post[b, :ORI, :128] = q1
        post[b, :ORI, 128:] = q2
        post[b, ORI:, :128] = q4
        post[b, ORI:, 128:] = q3

    def spread(first, count):
        def one(m, carry):
            for k in range(2):
                for half in range(2):
                    even = k == half
                    lanes = slice(half * 128, half * 128 + 128)
                    total = None
                    for b in range(4):
                        if b == 0 and not even:
                            continue
                        value = post[b, k * ORI : (k + 1) * ORI, lanes]
                        if b:
                            value = value * sums[m, pl.ds(b if even else 4 + b, 1), :]
                        total = value if total is None else total + value
                    back[m, k * ORI : (k + 1) * ORI, lanes] = total
            return carry

        lax.fori_loop(first, first + count, one, 0)

    spread(0, STEPS)
    find_codes()
    for copy in near:
        copy.wait_recv()
    peak, mass = merge_stats([stats_own[...]] + [stats_near[s] for s in range(3)])
    stats_mid[...] = jnp.concatenate([peak, mass, rest], axis=0)
    far = [put(stats_mid, stats_far.at[s], 44 + s, y_peers[s]) for s in range(7)]
    align(0, STEPS)
    choose(0, 12)
    for copy in far:
        copy.wait_recv()
    peak, mass = merge_stats([stats_mid[...]] + [stats_far[s] for s in range(7)])
    loglik = peak + jnp.log(mass)
    loglik_ref[...] = jnp.where(c == 0, loglik[:, :16], loglik[:, 16:32])
    scale = jnp.exp(own_peak - peak) / mass
    scale = jnp.concatenate([scale, scale], axis=1)

    def collect(m):
        grad = jnp.dot((back[m] * scale).astype(BF16), high[m], preferred_element_type=F32)
        out_real = grad[:ORI, :128] + sign * grad[ORI:, 128:]
        out_imag = grad[:ORI, 128:] - sign * grad[ORI:, :128]
        return jnp.concatenate([out_real, out_imag], axis=0)

    def insert(block, first, second):
        value = jnp.where(low, first, second)
        top = value.astype(BF16)
        left = jnp.concatenate([top, (value - top.astype(F32)).astype(BF16)], axis=0)
        out = jnp.dot(left, kernels[block], preferred_element_type=F32)
        out = out[: 2 * ORI] + out[2 * ORI :]
        at = lax.rem(block, 16) * 128 + (block // 16) * ORI
        rows = pl.ds(pl.multiple_of(at, ORI), ORI)
        inserted[rows, :] = jnp.concatenate([out[:ORI], out[ORI:]], axis=1).astype(BF16)

    def some_back(group, carry):
        for j in range(16):
            m = group * 16 + j
            folded[m] = collect(m)
        return carry

    lax.fori_loop(0, FREQ // 16, some_back, 0)
    folded[0] = folded[0] + collect(FREQ)
    get_kernels.wait()

    def some_insert(group, carry):
        for j in range(8):
            b = group * 8 + j
            insert(32 + b, folded[2 * b], pltpu.roll(folded[2 * b + 1], 64, 1))
            m = FREQ - 2 * b
            insert(b, pltpu.roll(folded[lax.rem(m, FREQ)], 64, 1), folded[m - 1])
        return carry

    lax.fori_loop(0, 4, some_insert, 0)

    def part_rows(xx, cc):
        return pl.ds(pl.multiple_of(xx * 384 + cc * 192, 192), 192)

    to_core = {}

    def scatter(s):
        xx = lax.rem(x + s, 4)
        rows = pl.ds(pl.multiple_of(xx * 384, 384), 384)
        part[rows, :] = jnp.dot(chosen[rows, :], inserted[...], preferred_element_type=F32)
        to_core[s] = put(part.at[part_rows(xx, 1 - c)], cores.at[s], 51 + s, core_peer)

    def both_cores(s):
        to_core[s].wait_recv()
        return part[part_rows(lax.rem(x + s, 4), c), :] + cores[s]

    steps = []

    def send_x(s):
        x_out[s - 1] = both_cores(s).astype(BF16)
        steps.append(put(x_out.at[s - 1], x_in.at[s - 1], 54 + s, x_peers[s - 1]))

    scatter(2)
    scatter(1)
    scatter(3)
    send_x(2)
    scatter(0)
    send_x(1)
    send_x(3)
    x_own[...] = both_cores(0)
    for copy in steps:
        copy.wait_recv()
    x_own[...] += sum(x_in[s].astype(F32) for s in range(3))
    for zz in range(8):
        rows = jnp.concatenate(
            [x_own[k * 64 + zz * 8 : k * 64 + zz * 8 + 8, :] for k in range(3)], axis=1
        )
        rows = jnp.concatenate([rows[:, :384], rows[:, 384:]], axis=0)
        z_own[zz] = rows
        z_out[zz] = rows.astype(BF16)
    steps = [
        put(z_out.at[lax.rem(z + s, 8)], z_in.at[s - 1], 57 + s, z_peers[s - 1])
        for s in range(1, 8)
    ]
    for copy in steps:
        copy.wait_recv()
    total = z_own[z]
    for s in range(7):
        total = total + z_in[s].astype(F32)
    for yy in range(8):
        for j in range(6):
            row = (j // 3) * 8 + yy
            y_out[yy, j : j + 1, :] = total[row : row + 1, (j % 3) * 128 : (j % 3) * 128 + 128]
        y_out[yy, 6:8, :] = jnp.zeros((2, 128), F32)
    steps = [
        put(y_out.at[lax.rem(y + s, 8)], y_in.at[s - 1], 64 + s, y_peers[s - 1])
        for s in range(1, 8)
    ]
    for copy in steps:
        copy.wait_recv()
    total = y_out[y]
    for s in range(7):
        total = total + y_in[s]
    for k in range(3):
        volume_ref[k] = total[2 * k : 2 * k + 2]
    for copy in sends:
        copy.wait_send()


def finish_kernel(volume, loglik, volume_ref, loglik_ref):
    volume_ref[...] = volume[...]
    loglik_ref[...] = loglik[...]


def shards(images, slices, noise_weight, shifts, kernels, targets):
    trig, sums = tables()
    trig_t = np.repeat(np.concatenate([trig, trig], axis=1).T, IMGS, axis=1)
    in_vmem = pl.BlockSpec(memory_space=pltpu.VMEM)
    in_smem = pl.BlockSpec(memory_space=pltpu.SMEM)
    anywhere = pl.BlockSpec(memory_space=pl.ANY)
    volume, loglik = pl.pallas_call(
        step_kernel,
        out_shape=(
            jax.ShapeDtypeStruct((3, 2, 128), F32),
            jax.ShapeDtypeStruct((1, 16), F32),
        ),
        in_specs=[
            anywhere, anywhere, in_vmem, in_smem, anywhere, in_vmem, in_vmem, anywhere, anywhere,
        ],
        out_specs=(in_vmem, in_vmem),
        scratch_shapes=[
            pltpu.VMEM((16, 2, PIX), BF16),
            pltpu.VMEM((2, 2, PIX), BF16),
            pltpu.VMEM((64, 128, 128), BF16),
            pltpu.VMEM((STEPS, 8, 128), F32),
            pltpu.VMEM((FREQ, 256), F32),
            pltpu.VMEM((FREQ * 16, 128), F32),
            pltpu.VMEM((FREQ * 16, 128), F32),
            pltpu.VMEM((FREQ, IMGS, 256), BF16),
            pltpu.VMEM((16, 2, FREQ, 256), BF16),
            pltpu.VMEM((72, 128), F32),
            pltpu.VMEM((256, 256), F32),
            pltpu.VMEM((STEPS, 256, 256), BF16),
            pltpu.VMEM((STEPS, 256, 256), BF16),
            pltpu.VMEM((STEPS, 256, 256), BF16),
            pltpu.VMEM((ORI * FREQ, 128), F32),
            pltpu.VMEM((ORI * FREQ, 128), F32),
            pltpu.VMEM((ORI, 128), F32),
            pltpu.VMEM((4, 2 * ORI, 256), F32),
            pltpu.VMEM((14, ORI, 128), F32),
            pltpu.VMEM((16, 128), F32),
            pltpu.VMEM((16, 128), F32),
            pltpu.VMEM((1536, 2048), BF16),
            pltpu.VMEM((4, 2 * ORI, 256), F32),
            pltpu.VMEM((STEPS, 2 * ORI, 256), F32),
            pltpu.VMEM((FREQ, 2 * ORI, 128), F32),
            pltpu.VMEM((FREQ * ORI, 256), BF16),
            pltpu.VMEM((1536, 256), F32),
            pltpu.VMEM((4, 192, 256), F32),
            pltpu.VMEM((8, 128), F32),
            pltpu.VMEM((3, 8, 128), F32),
            pltpu.VMEM((8, 128), F32),
            pltpu.VMEM((7, 8, 128), F32),
            pltpu.VMEM((3, 192, 256), BF16),
            pltpu.VMEM((3, 192, 256), BF16),
            pltpu.VMEM((192, 256), F32),
            pltpu.VMEM((8, 16, 384), BF16),
            pltpu.VMEM((7, 16, 384), BF16),
            pltpu.VMEM((8, 16, 384), F32),
            pltpu.VMEM((8, 8, 128), F32),
            pltpu.VMEM((7, 8, 128), F32),
            pltpu.SemaphoreType.DMA((72,)),
            pltpu.SemaphoreType.DMA((72,)),
            pltpu.SemaphoreType.DMA((5,)),
        ],
        compiler_params=pltpu.CompilerParams(
            vmem_limit_bytes=VMEM_LIMIT, collective_id=0, has_side_effects=True
        ),
        name="expectation_step",
    )(
        images, slices, noise_weight.reshape(64, 128), shifts.T, kernels, targets,
        jnp.asarray(trig), jnp.asarray(sums), jnp.asarray(trig_t),
    )
    volume, loglik = pl.pallas_call(
        finish_kernel,
        out_shape=(
            jax.ShapeDtypeStruct((3, 2, 128), F32),
            jax.ShapeDtypeStruct((1, 16), F32),
        ),
        in_specs=[in_vmem, in_vmem],
        out_specs=(in_vmem, in_vmem),
        name="finish",
    )(volume, loglik)
    return volume, loglik.reshape(16)


def solution(mesh):
    placed = (
        P("dom", None, None),
        P(("orient", "dom"), None, None),
        P(),
        P(),
        P(),
        P("orient", None),
    )
    return jax.shard_map(
        shards,
        mesh=mesh,
        in_specs=placed,
        out_specs=(P(("dom", "orient"), None, None), P("dom")),
        check_vma=False,
    )
```

```python
import jax
import jax.numpy as jnp
import numpy as np
from jax import lax
from jax.experimental import pallas as pl
from jax.experimental.pallas import tpu as pltpu
from jax.sharding import PartitionSpec as P

F32 = jnp.float32
BF16 = jnp.bfloat16
MESH = pl.DeviceIdType.MESH
PIX = 8192
TRANS = 49
FREQ = 64
IMGS = 32
ORI = 32
STEPS = FREQ + 1
VMEM_LIMIT = 56 * 1024 * 1024


def tables():
    kx = np.arange(64)
    unit = 2.0 * np.pi / 128.0
    rows = np.zeros((8, 128), np.float32)
    for a in range(4):
        rows[a, :64] = rows[a, 64:] = np.cos(unit * a * kx)
    for a in range(1, 4):
        rows[4 + a, :64] = np.sin(unit * a * kx)
        rows[4 + a, 64:] = -np.sin(unit * a * kx)
    m = np.arange(STEPS)
    sums = np.zeros((STEPS, 8, 128), np.float32)
    for b in range(4):
        sums[:, b, :] = np.cos(unit * b * m)[:, None]
        sums[:, 4 + b, :] = np.where(m == 64, 0.0, np.sin(unit * b * m))[:, None]
    return rows, sums


def repeat(first, count, step, wide=8):
    def some(group, carry):
        for j in range(wide):
            step(first + group * wide + j)
        return carry

    lax.fori_loop(0, count // wide, some, 0)
    for j in range(count - count % wide, count):
        step(first + j)


def entry_of(sigma, shift_y):
    return (0 if sigma > 0 else 7) + shift_y + 3


def fold_pair(m, block, low):
    if m % 2 == 0:
        first = block(32 + m // 2)
        second = pltpu.roll(block(32 - m // 2 if m else 0), 64, 1)
    else:
        first = pltpu.roll(block(32 + (m - 1) // 2), 64, 1)
        second = block(32 - (m + 1) // 2)
    return jnp.where(low, first, second)


def aligned_rows(pair, factors):
    real, imag = pair[:, :128], pair[:, 128:]
    rows = []
    for r in range(8):
        row = factors[r : r + 1]
        if r == 4:
            rows.append(jnp.zeros((IMGS, 256), F32))
        else:
            rows.append(jnp.concatenate([real * row, imag * row], axis=1))
    return rows


def merge_stats(stats):
    peak = stats[0][0:1]
    for part in stats[1:]:
        peak = jnp.maximum(peak, part[0:1])
    mass = jnp.zeros_like(peak)
    for part in stats:
        mass = mass + part[1:2] * jnp.exp(part[0:1] - peak)
    return peak, mass


def step_kernel(
    images_hbm, slices_hbm, noise_weight, shifts, kernels_hbm, targets, trig, sums_hbm, trig_t_hbm,
    volume_ref, loglik_ref,
    images_raw, slices_raw, kernels, sums,
    fold_rows, image_real, image_imag, images, slices, weight, trig_t, high, high_t, low_t, real, imag, energy, acc, expo,
    counts, codes, chosen, post, back, folded, inserted, part, cores,
    stats_own, stats_near, stats_mid, stats_far,
    x_out, x_in, x_own, z_out, z_in, z_own, y_out, y_in,
    send, recv, local,
):
    dom, ori = lax.axis_index("dom"), lax.axis_index("orient")
    c, zh, x = dom % 2, (dom // 2) % 4, dom // 8
    y, zl = ori // 2, ori % 2
    z = zh * 2 + zl

    def dev(dx, dz, dc, dy):
        xx, zz, yy = lax.rem(x + dx, 4), lax.rem(z + dz, 8), lax.rem(y + dy, 8)
        cc = 1 - c if dc else c
        return (xx * 8 + (zz // 2) * 2 + cc, yy * 2 + zz % 2)

    def dev_zl(dl, dc):
        cc = 1 - c if dc else c
        ll = 1 - zl if dl else zl
        return (x * 8 + zh * 2 + cc, y * 2 + ll)

    core_peer = dev(0, 0, 1, 0)
    x_peers = [dev(s, 0, 0, 0) for s in range(1, 4)]
    z_peers = [dev(0, s, 0, 0) for s in range(1, 8)]
    y_peers = [dev(0, 0, 0, s) for s in range(1, 8)]
    near_peers = [core_peer, dev_zl(1, 0), dev_zl(1, 1)]
    barrier = pltpu.get_barrier_semaphore()
    everyone = [core_peer, near_peers[2]] + x_peers + z_peers + y_peers
    for peer in everyone:
        pl.semaphore_signal(barrier, inc=1, device_id=peer, device_id_type=MESH)

    get_slices = pltpu.make_async_copy(slices_hbm, slices_raw, local.at[0])
    get_slices.start()
    get_images = pltpu.make_async_copy(images_hbm, images_raw, local.at[1])
    get_images.start()
    get_kernels = pltpu.make_async_copy(kernels_hbm, kernels, local.at[2])
    get_kernels.start()
    get_sums = pltpu.make_async_copy(sums_hbm, sums, local.at[3])
    get_sums.start()
    get_trig_t = pltpu.make_async_copy(trig_t_hbm, trig_t, local.at[4])
    get_trig_t.start()

    sends = []

    def put(src, dst, sem, peer):
        copy = pltpu.make_async_remote_copy(
            src_ref=src, dst_ref=dst, send_sem=send.at[sem], recv_sem=recv.at[sem],
            device_id=peer, device_id_type=MESH,
        )
        copy.start()
        sends.append(copy)
        return copy

    def got(ref, sem):
        pltpu.make_async_remote_copy(
            src_ref=ref, dst_ref=ref, send_sem=send.at[sem], recv_sem=recv.at[sem],
            device_id=core_peer, device_id_type=MESH,
        ).wait_recv()

    low = lax.broadcasted_iota(jnp.int32, (1, 128), 1) < 64
    sign = jnp.where(low, 1.0, -1.0).astype(F32)

    get_slices.wait()
    for j in range(2):
        for m in range(FREQ):
            both = fold_pair(
                m, lambda b: slices_raw[j, :, b * 128 : b * 128 + 128].astype(F32), low
            )
            fold_rows[m : m + 1, :128] = both[0:1]
            fold_rows[m : m + 1, 128:] = both[1:2]
        slices[0, j] = fold_rows[...].astype(BF16)

    def fold_images(first, count):
        def one(i, carry):
            for m in range(FREQ):
                both = fold_pair(
                    m, lambda b: images_raw[i, :, b * 128 : b * 128 + 128].astype(F32), low
                )
                row = pl.ds(m * 16 + i, 1)
                image_real[row, :] = both[0:1]
                image_imag[row, :] = both[1:2]
            return carry

        lax.fori_loop(first, first + count, one, 0)

    def image_half(cc):
        return pl.ds(pl.multiple_of(cc * 16, 16), 16)

    def send_images():
        def one(m):
            at = pl.ds(pl.multiple_of(m * 16, 16), 16)
            rows = jnp.concatenate([image_real[at, :], image_imag[at, :]], axis=1)
            images[m, image_half(c), :] = rows.astype(BF16)

        repeat(0, FREQ, one)
        here = images.at[:, image_half(c)]
        put(here, here, 0, core_peer)

    def fold_weight():
        for m in range(FREQ):
            row = fold_pair(m, lambda b: noise_weight[b : b + 1, :], low)
            if m == 0:
                weight[FREQ : FREQ + 1, :] = jnp.where(low, 0.0, row)
                row = jnp.where(low, row, 0.0)
            weight[m : m + 1, :] = row

    def count_cells():
        row = lax.broadcasted_iota(jnp.int32, (16, 128), 0)
        size = lax.broadcasted_iota(jnp.int32, (16, 128), 1) // IMGS
        total = jnp.zeros((16, 128), F32)
        for t in range(TRANS):
            shift_x, shift_y = shifts[0, t], shifts[1, t]
            at = jnp.where(shift_x >= 0, 3, 10) + shift_y
            hit = (row == at) & (size == jnp.abs(shift_x))
            total = total + jnp.where(hit, 1.0, 0.0)
        counts[...] = total

    def find_codes():
        block = targets[...]
        owner = (block * 43691) >> 17
        k = block - 3 * owner
        core_at, z_hi_at, x_at = (owner >> 4) & 1, (owner >> 5) & 3, owner >> 7
        y_at, z_lo_at = (owner >> 1) & 7, owner & 1
        code = (x_at * 2 + core_at) * 192 + k * 64 + (z_hi_at * 2 + z_lo_at) * 8 + y_at
        row = lax.broadcasted_iota(jnp.int32, (64, ORI), 0)
        mine = lax.broadcasted_iota(jnp.int32, (64, ORI), 1)
        x_from = (x + (mine >> 3)) & 3
        z_from = (zh + (mine >> 1)) & 3
        source = ((x_from * 4 + z_from) * 2 + c) * 2 + (mine & 1)
        pick = jnp.where(row == source, 1.0, 0.0).astype(BF16)
        dims = (((0,), (0,)), ((), ()))
        upper, lower = (code >> 5).astype(F32), (code & 31).astype(F32)
        upper = lax.dot_general(upper.astype(BF16), pick, dims, preferred_element_type=F32)
        lower = lax.dot_general(lower.astype(BF16), pick, dims, preferred_element_type=F32)
        code = upper * 32.0 + lower
        codes[...] = jnp.concatenate([code[16 * q : 16 * q + 16] for q in range(4)], axis=1)

    def choose(first, count):
        def one(t, carry):
            rows = lax.broadcasted_iota(jnp.int32, (128, 128), 0).astype(F32)
            rows = rows + (t * 128).astype(F32)
            at = pl.ds(pl.multiple_of(t * 128, 128), 128)
            for j in range(16):
                hit = rows == codes[j : j + 1, :]
                chosen[at, j * 128 : j * 128 + 128] = jnp.where(hit, 1.0, 0.0).astype(BF16)
            return carry

        lax.fori_loop(first, first + count, one, 0)

    def wait_images():
        got(images.at[:, image_half(1 - c)], 0)

    spread_images = jnp.where(
        lax.broadcasted_iota(jnp.int32, (2 * IMGS, 256), 0) % IMGS
        == lax.broadcasted_iota(jnp.int32, (2 * IMGS, 256), 1) % IMGS,
        1.0,
        0.0,
    ).astype(BF16)

    def align(first, count):
        def one(m):
            factors = trig[...] * weight[pl.ds(m, 1), :]
            rows = aligned_rows(images[lax.rem(m, FREQ)].astype(F32), factors)
            for r, row in enumerate(rows):
                high[m, r * IMGS : (r + 1) * IMGS, :] = row.astype(BF16)

        repeat(first, count, one)

    def align_turned(first, count):
        def one(m):
            w = weight[pl.ds(m, 1), :]
            pair = images[lax.rem(m, FREQ)].astype(F32) * jnp.concatenate([w, w], axis=1)
            top = pair.astype(BF16)
            terms = jnp.concatenate([top, (pair - top.astype(F32)).astype(BF16)], axis=0)
            turned = lax.dot_general(
                terms, spread_images, (((0,), (0,)), ((), ())), preferred_element_type=F32
            )
            turned = turned * trig_t[...]
            top = turned.astype(BF16)
            high_t[m] = top
            low_t[m] = (turned - top.astype(F32)).astype(BF16)

        repeat(first, count, one)

    def piece(dx, dz, h):
        return slices.at[dx * 4 + dz, :, pl.ds(h * 32, 32)]

    def single(dx, dz, h, j):
        return slices.at[dx * 4 + dz, j, pl.ds(h * 32, 32)]

    def gsem(kind, h):
        return 1 + kind * 2 + h

    z_up, z_down = z_peers[1], z_peers[5]

    def along_z(h):
        put(piece(0, 0, h), piece(0, 3, h), gsem(0, h), z_up)
        put(piece(0, 0, h), piece(0, 1, h), gsem(1, h), z_down)

    def along_x(dz, h):
        for s in range(1, 4):
            put(piece(0, dz, h), piece(4 - s, dz, h), gsem(3 + 3 * dz + s, h), x_peers[s - 1])

    def pass_z(h):
        got(piece(0, 3, h), gsem(0, h))
        put(single(0, 3, h, 0), single(0, 2, h, 0), gsem(2, h), z_up)
        got(piece(0, 1, h), gsem(1, h))
        put(single(0, 1, h, 1), single(0, 2, h, 1), gsem(3, h), z_down)

    def far_z(h):
        got(single(0, 2, h, 0), gsem(2, h))
        got(single(0, 2, h, 1), gsem(3, h))

    def got_x(h):
        for dz in (0, 3, 1, 2):
            for s in range(1, 4):
                got(piece(4 - s, dz, h), gsem(3 + 3 * dz + s, h))

    pl.semaphore_wait(barrier, len(everyone))
    for h in range(2):
        along_z(h)
        along_x(0, h)
    get_images.wait()
    fold_images(0, 16)
    send_images()
    fold_weight()
    count_cells()
    pass_z(0)
    along_x(3, 0)
    along_x(1, 0)
    pass_z(1)
    along_x(3, 1)
    wait_images()
    get_trig_t.wait()
    align_turned(0, 16)
    far_z(0)
    along_x(2, 0)
    along_x(1, 1)
    far_z(1)
    along_x(2, 1)
    align_turned(16, STEPS - 16)
    get_sums.wait()

    acc[...] = jnp.zeros_like(acc)
    energy[...] = jnp.zeros_like(energy)

    def widen(h):
        def one(o):
            block = slices[o // 2, lax.rem(o, 2), pl.ds(h * 32, 32), :].astype(F32)
            rows = pl.ds(pl.multiple_of(o * FREQ + h * 32, 32), 32)
            real[rows, :] = block[:, :128]
            imag[rows, :] = block[:, 128:]

        repeat(0, ORI, one)

    def correlate(m, src):
        at = pl.ds(src, ORI, stride=FREQ)
        s_r, s_i = real[at, :], imag[at, :]
        energy[...] += weight[pl.ds(m, 1), :] * (s_r * s_r + s_i * s_i)
        left = jnp.concatenate(
            [
                jnp.concatenate([s_r, s_i], axis=1),
                jnp.concatenate([-sign * s_i, sign * s_r], axis=1),
            ],
            axis=0,
        ).astype(BF16)
        return jnp.dot(left, high_t[m], preferred_element_type=F32) + jnp.dot(
            left, low_t[m], preferred_element_type=F32
        )

    def add_scores(parts):
        for b in range(4):
            for k in range(2):
                for half in range(2):
                    even = k == half
                    if b == 0 and not even:
                        continue
                    lanes = slice(half * 128, half * 128 + 128)
                    total = acc[b, k * ORI : (k + 1) * ORI, lanes]
                    for m, value in parts:
                        value = value[k * ORI : (k + 1) * ORI, lanes]
                        if b:
                            value = value * sums[m, pl.ds(b if even else 4 + b, 1), :]
                        total = total + value
                    acc[b, k * ORI : (k + 1) * ORI, lanes] = total

    def score_half(h):
        widen(h)

        def some(group, carry):
            steps = [h * 32 + group * 8 + j for j in range(8)]
            add_scores([(m, correlate(m, m)) for m in steps])
            return carry

        lax.fori_loop(0, 4, some, 0)

    got_x(0)
    score_half(0)
    add_scores([(FREQ, correlate(FREQ, 0))])
    got_x(1)
    score_half(1)

    half_energy = 0.5 * jnp.sum(energy[...], axis=1, keepdims=True)
    peak = jnp.full((ORI, 128), -1e30, F32)
    for b in range(4):
        q1 = acc[b, :ORI, :128] - half_energy
        q2 = acc[b, :ORI, 128:]
        q4 = acc[b, ORI:, :128]
        q3 = acc[b, ORI:, 128:]
        for tau in (1, -1) if b else (1,):
            for sigma in (1, -1):
                entry = entry_of(sigma, tau * b)
                value = q1 - sigma * q3
                if b:
                    value = value - tau * (sigma * q2 + q4)
                expo[entry] = value
                live = counts[entry : entry + 1, :] > 0
                peak = jnp.maximum(peak, jnp.where(live, value, -1e30))
    peak = jnp.max(peak, axis=0, keepdims=True)
    peak = jnp.maximum(peak, pltpu.roll(peak, 32, 1))
    peak = jnp.maximum(peak, pltpu.roll(peak, 64, 1))
    mass = jnp.zeros((ORI, 128), F32)
    for entry in range(14):
        count = counts[entry : entry + 1, :]
        value = jnp.where(count > 0, expo[entry] - peak, -1e30)
        value = jnp.exp(value) * count
        expo[entry] = value
        mass = mass + value
    mass = jnp.sum(mass, axis=0, keepdims=True)
    mass = mass + pltpu.roll(mass, 32, 1)
    mass = mass + pltpu.roll(mass, 64, 1)
    own_peak = peak
    rest = jnp.zeros((6, 128), F32)
    stats_own[...] = jnp.concatenate([peak, mass, rest], axis=0)

    near = [put(stats_own, stats_near.at[s], 41 + s, near_peers[s]) for s in range(3)]
    for b in range(4):
        q1 = jnp.zeros((ORI, 128), F32)
        q2, q3, q4 = q1, q1, q1
        for tau in (1, -1) if b else (1,):
            for sigma in (1, -1):
                value = expo[entry_of(sigma, tau * b)]
                q1 = q1 + value
                q2 = q2 - (sigma * tau) * value
                q3 = q3 - sigma * value
                q4 = q4 - tau * value
        post[b, :ORI, :128] = q1
        post[b, :ORI, 128:] = q2
        post[b, ORI:, :128] = q4
        post[b, ORI:, 128:] = q3

    def spread(first, count):
        def one(m):
            for k in range(2):
                for half in range(2):
                    even = k == half
                    lanes = slice(half * 128, half * 128 + 128)
                    total = None
                    for b in range(4):
                        if b == 0 and not even:
                            continue
                        value = post[b, k * ORI : (k + 1) * ORI, lanes]
                        if b:
                            value = value * sums[m, pl.ds(b if even else 4 + b, 1), :]
                        total = value if total is None else total + value
                    back[m, k * ORI : (k + 1) * ORI, lanes] = total

        repeat(first, count, one, 4)

    spread(0, STEPS)
    find_codes()
    for copy in near:
        copy.wait_recv()
    peak, mass = merge_stats([stats_own[...]] + [stats_near[s] for s in range(3)])
    stats_mid[...] = jnp.concatenate([peak, mass, rest], axis=0)
    far = [put(stats_mid, stats_far.at[s], 44 + s, y_peers[s]) for s in range(7)]
    align(0, STEPS)
    choose(0, 12)
    for copy in far:
        copy.wait_recv()
    peak, mass = merge_stats([stats_mid[...]] + [stats_far[s] for s in range(7)])
    loglik = peak + jnp.log(mass)
    loglik_ref[...] = jnp.where(c == 0, loglik[:, :16], loglik[:, 16:32])
    scale = jnp.exp(own_peak - peak) / mass
    scale = jnp.concatenate([scale, scale], axis=1)

    def collect(m):
        grad = jnp.dot((back[m] * scale).astype(BF16), high[m], preferred_element_type=F32)
        out_real = grad[:ORI, :128] + sign * grad[ORI:, 128:]
        out_imag = grad[:ORI, 128:] - sign * grad[ORI:, :128]
        return jnp.concatenate([out_real, out_imag], axis=0)

    def insert(block, first, second):
        value = jnp.where(low, first, second)
        top = value.astype(BF16)
        left = jnp.concatenate([top, (value - top.astype(F32)).astype(BF16)], axis=0)
        out = jnp.dot(left, kernels[block], preferred_element_type=F32)
        out = out[: 2 * ORI] + out[2 * ORI :]
        at = lax.rem(block, 16) * 128 + (block // 16) * ORI
        rows = pl.ds(pl.multiple_of(at, ORI), ORI)
        inserted[rows, :] = jnp.concatenate([out[:ORI], out[ORI:]], axis=1).astype(BF16)

    def some_back(group, carry):
        for j in range(16):
            m = group * 16 + j
            folded[m] = collect(m)
        return carry

    lax.fori_loop(0, FREQ // 16, some_back, 0)
    folded[0] = folded[0] + collect(FREQ)
    get_kernels.wait()

    def some_insert(group, carry):
        for j in range(8):
            b = group * 8 + j
            insert(32 + b, folded[2 * b], pltpu.roll(folded[2 * b + 1], 64, 1))
            m = FREQ - 2 * b
            insert(b, pltpu.roll(folded[lax.rem(m, FREQ)], 64, 1), folded[m - 1])
        return carry

    lax.fori_loop(0, 4, some_insert, 0)

    def part_rows(xx, cc):
        return pl.ds(pl.multiple_of(xx * 384 + cc * 192, 192), 192)

    to_core = {}

    def scatter(s):
        xx = lax.rem(x + s, 4)
        rows = pl.ds(pl.multiple_of(xx * 384, 384), 384)
        part[rows, :] = jnp.dot(chosen[rows, :], inserted[...], preferred_element_type=F32)
        to_core[s] = put(part.at[part_rows(xx, 1 - c)], cores.at[s], 51 + s, core_peer)

    def both_cores(s):
        to_core[s].wait_recv()
        return part[part_rows(lax.rem(x + s, 4), c), :] + cores[s]

    steps = []

    def send_x(s):
        x_out[s - 1] = both_cores(s).astype(BF16)
        steps.append(put(x_out.at[s - 1], x_in.at[s - 1], 54 + s, x_peers[s - 1]))

    scatter(2)
    scatter(1)
    scatter(3)
    send_x(2)
    scatter(0)
    send_x(1)
    send_x(3)
    x_own[...] = both_cores(0)
    for copy in steps:
        copy.wait_recv()
    x_own[...] += sum(x_in[s].astype(F32) for s in range(3))
    for zz in range(8):
        rows = jnp.concatenate(
            [x_own[k * 64 + zz * 8 : k * 64 + zz * 8 + 8, :] for k in range(3)], axis=1
        )
        rows = jnp.concatenate([rows[:, :384], rows[:, 384:]], axis=0)
        z_own[zz] = rows
        z_out[zz] = rows.astype(BF16)
    steps = [
        put(z_out.at[lax.rem(z + s, 8)], z_in.at[s - 1], 57 + s, z_peers[s - 1])
        for s in range(1, 8)
    ]
    for copy in steps:
        copy.wait_recv()
    total = z_own[z]
    for s in range(7):
        total = total + z_in[s].astype(F32)
    for yy in range(8):
        for j in range(6):
            row = (j // 3) * 8 + yy
            y_out[yy, j : j + 1, :] = total[row : row + 1, (j % 3) * 128 : (j % 3) * 128 + 128]
        y_out[yy, 6:8, :] = jnp.zeros((2, 128), F32)
    steps = [
        put(y_out.at[lax.rem(y + s, 8)], y_in.at[s - 1], 64 + s, y_peers[s - 1])
        for s in range(1, 8)
    ]
    for copy in steps:
        copy.wait_recv()
    total = y_out[y]
    for s in range(7):
        total = total + y_in[s]
    for k in range(3):
        volume_ref[k] = total[2 * k : 2 * k + 2]
    for copy in sends:
        copy.wait_send()


def finish_kernel(volume, loglik, volume_ref, loglik_ref):
    volume_ref[...] = volume[...]
    loglik_ref[...] = loglik[...]


def shards(images, slices, noise_weight, shifts, kernels, targets):
    trig, sums = tables()
    trig_t = np.repeat(np.concatenate([trig, trig], axis=1).T, IMGS, axis=1)
    in_vmem = pl.BlockSpec(memory_space=pltpu.VMEM)
    in_smem = pl.BlockSpec(memory_space=pltpu.SMEM)
    anywhere = pl.BlockSpec(memory_space=pl.ANY)
    volume, loglik = pl.pallas_call(
        step_kernel,
        out_shape=(
            jax.ShapeDtypeStruct((3, 2, 128), F32),
            jax.ShapeDtypeStruct((1, 16), F32),
        ),
        in_specs=[
            anywhere, anywhere, in_vmem, in_smem, anywhere, in_vmem, in_vmem, anywhere, anywhere,
        ],
        out_specs=(in_vmem, in_vmem),
        scratch_shapes=[
            pltpu.VMEM((16, 2, PIX), BF16),
            pltpu.VMEM((2, 2, PIX), BF16),
            pltpu.VMEM((64, 128, 128), BF16),
            pltpu.VMEM((STEPS, 8, 128), F32),
            pltpu.VMEM((FREQ, 256), F32),
            pltpu.VMEM((FREQ * 16, 128), F32),
            pltpu.VMEM((FREQ * 16, 128), F32),
            pltpu.VMEM((FREQ, IMGS, 256), BF16),
            pltpu.VMEM((16, 2, FREQ, 256), BF16),
            pltpu.VMEM((72, 128), F32),
            pltpu.VMEM((256, 256), F32),
            pltpu.VMEM((STEPS, 256, 256), BF16),
            pltpu.VMEM((STEPS, 256, 256), BF16),
            pltpu.VMEM((STEPS, 256, 256), BF16),
            pltpu.VMEM((ORI * FREQ, 128), F32),
            pltpu.VMEM((ORI * FREQ, 128), F32),
            pltpu.VMEM((ORI, 128), F32),
            pltpu.VMEM((4, 2 * ORI, 256), F32),
            pltpu.VMEM((14, ORI, 128), F32),
            pltpu.VMEM((16, 128), F32),
            pltpu.VMEM((16, 128), F32),
            pltpu.VMEM((1536, 2048), BF16),
            pltpu.VMEM((4, 2 * ORI, 256), F32),
            pltpu.VMEM((STEPS, 2 * ORI, 256), F32),
            pltpu.VMEM((FREQ, 2 * ORI, 128), F32),
            pltpu.VMEM((FREQ * ORI, 256), BF16),
            pltpu.VMEM((1536, 256), F32),
            pltpu.VMEM((4, 192, 256), F32),
            pltpu.VMEM((8, 128), F32),
            pltpu.VMEM((3, 8, 128), F32),
            pltpu.VMEM((8, 128), F32),
            pltpu.VMEM((7, 8, 128), F32),
            pltpu.VMEM((3, 192, 256), BF16),
            pltpu.VMEM((3, 192, 256), BF16),
            pltpu.VMEM((192, 256), F32),
            pltpu.VMEM((8, 16, 384), BF16),
            pltpu.VMEM((7, 16, 384), BF16),
            pltpu.VMEM((8, 16, 384), F32),
            pltpu.VMEM((8, 8, 128), F32),
            pltpu.VMEM((7, 8, 128), F32),
            pltpu.SemaphoreType.DMA((72,)),
            pltpu.SemaphoreType.DMA((72,)),
            pltpu.SemaphoreType.DMA((5,)),
        ],
        compiler_params=pltpu.CompilerParams(
            vmem_limit_bytes=VMEM_LIMIT, collective_id=0, has_side_effects=True
        ),
        name="expectation_step",
    )(
        images, slices, noise_weight.reshape(64, 128), shifts.T, kernels, targets,
        jnp.asarray(trig), jnp.asarray(sums), jnp.asarray(trig_t),
    )
    volume, loglik = pl.pallas_call(
        finish_kernel,
        out_shape=(
            jax.ShapeDtypeStruct((3, 2, 128), F32),
            jax.ShapeDtypeStruct((1, 16), F32),
        ),
        in_specs=[in_vmem, in_vmem],
        out_specs=(in_vmem, in_vmem),
        name="finish",
    )(volume, loglik)
    return volume, loglik.reshape(16)


def solution(mesh):
    placed = (
        P("dom", None, None),
        P(("orient", "dom"), None, None),
        P(),
        P(),
        P(),
        P("orient", None),
    )
    return jax.shard_map(
        shards,
        mesh=mesh,
        in_specs=placed,
        out_specs=(P(("dom", "orient"), None, None), P("dom")),
        check_vma=False,
    )
```

```python
import jax
import jax.numpy as jnp
import numpy as np
from jax import lax
from jax.experimental import pallas as pl
from jax.experimental.pallas import tpu as pltpu
from jax.sharding import PartitionSpec as P

F32 = jnp.float32
BF16 = jnp.bfloat16
MESH = pl.DeviceIdType.MESH
PIX = 8192
TRANS = 49
FREQ = 64
IMGS = 32
ORI = 32
STEPS = FREQ + 1
VMEM_LIMIT = 56 * 1024 * 1024


def tables():
    kx = np.arange(64)
    unit = 2.0 * np.pi / 128.0
    rows = np.zeros((8, 128), np.float32)
    for a in range(4):
        rows[a, :64] = rows[a, 64:] = np.cos(unit * a * kx)
    for a in range(1, 4):
        rows[4 + a, :64] = np.sin(unit * a * kx)
        rows[4 + a, 64:] = -np.sin(unit * a * kx)
    m = np.arange(STEPS)
    sums = np.zeros((STEPS, 8, 128), np.float32)
    for b in range(4):
        sums[:, b, :] = np.cos(unit * b * m)[:, None]
        sums[:, 4 + b, :] = np.where(m == 64, 0.0, np.sin(unit * b * m))[:, None]
    return rows, sums


def repeat(first, count, step, wide=8):
    def some(group, carry):
        for j in range(wide):
            step(first + group * wide + j)
        return carry

    lax.fori_loop(0, count // wide, some, 0)
    for j in range(count - count % wide, count):
        step(first + j)


def entry_of(sigma, shift_y):
    return (0 if sigma > 0 else 7) + shift_y + 3


def fold_pair(m, block, low):
    if m % 2 == 0:
        first = block(32 + m // 2)
        second = pltpu.roll(block(32 - m // 2 if m else 0), 64, 1)
    else:
        first = pltpu.roll(block(32 + (m - 1) // 2), 64, 1)
        second = block(32 - (m + 1) // 2)
    return jnp.where(low, first, second)


def aligned_rows(pair, factors):
    real, imag = pair[:, :128], pair[:, 128:]
    rows = []
    for r in range(8):
        row = factors[r : r + 1]
        if r == 4:
            rows.append(jnp.zeros((IMGS, 256), F32))
        else:
            rows.append(jnp.concatenate([real * row, imag * row], axis=1))
    return rows


def merge_stats(stats):
    peak = stats[0][0:1]
    for part in stats[1:]:
        peak = jnp.maximum(peak, part[0:1])
    mass = jnp.zeros_like(peak)
    for part in stats:
        mass = mass + part[1:2] * jnp.exp(part[0:1] - peak)
    return peak, mass


def step_kernel(
    images_hbm, slices_hbm, noise_weight, shifts, kernels_hbm, targets, trig, sums_hbm, trig_t_hbm,
    volume_ref, loglik_ref,
    images_raw, slices_raw, kernels, sums,
    fold_rows, image_real, image_imag, images, slices, weight, trig_t, high, high_t, low_t, real, imag, energy, acc, expo,
    counts, codes, chosen, post, back, folded, inserted, part, cores,
    stats_own, stats_near, stats_mid, stats_far,
    x_out, x_in, x_own, z_out, z_in, z_own, y_out, y_in,
    send, recv, local, heard,
):
    dom, ori = lax.axis_index("dom"), lax.axis_index("orient")
    c, zh, x = dom % 2, (dom // 2) % 4, dom // 8
    y, zl = ori // 2, ori % 2
    z = zh * 2 + zl

    def dev(dx, dz, dc, dy):
        xx, zz, yy = lax.rem(x + dx, 4), lax.rem(z + dz, 8), lax.rem(y + dy, 8)
        cc = 1 - c if dc else c
        return (xx * 8 + (zz // 2) * 2 + cc, yy * 2 + zz % 2)

    def dev_zl(dl, dc):
        cc = 1 - c if dc else c
        ll = 1 - zl if dl else zl
        return (x * 8 + zh * 2 + cc, y * 2 + ll)

    core_peer = dev(0, 0, 1, 0)
    x_peers = [dev(s, 0, 0, 0) for s in range(1, 4)]
    z_peers = [dev(0, s, 0, 0) for s in range(1, 8)]
    y_peers = [dev(0, 0, 0, s) for s in range(1, 8)]
    near_peers = [core_peer, dev_zl(1, 0), dev_zl(1, 1)]
    barrier = pltpu.get_barrier_semaphore()
    everyone = [core_peer, near_peers[1], z_peers[1], z_peers[5], y_peers[0], y_peers[6]]
    everyone += x_peers
    for peer in everyone:
        pl.semaphore_signal(barrier, inc=1, device_id=peer, device_id_type=MESH)

    get_slices = pltpu.make_async_copy(slices_hbm, slices_raw, local.at[0])
    get_slices.start()
    get_images = pltpu.make_async_copy(images_hbm, images_raw, local.at[1])
    get_images.start()
    get_kernels = pltpu.make_async_copy(kernels_hbm, kernels, local.at[2])
    get_kernels.start()
    get_sums = pltpu.make_async_copy(sums_hbm, sums, local.at[3])
    get_sums.start()
    get_trig_t = pltpu.make_async_copy(trig_t_hbm, trig_t, local.at[4])
    get_trig_t.start()

    def hear_of_y():
        for step in range(3):
            pl.semaphore_signal(
                heard.at[step], inc=1, device_id=y_peers[0], device_id_type=MESH
            )
            pl.semaphore_signal(
                heard.at[3 + step], inc=1, device_id=y_peers[6], device_id_type=MESH
            )
            yield
            pl.semaphore_wait(heard.at[step], 1)
            pl.semaphore_wait(heard.at[3 + step], 1)
        yield

    sends = []

    def put(src, dst, sem, peer):
        copy = pltpu.make_async_remote_copy(
            src_ref=src, dst_ref=dst, send_sem=send.at[sem], recv_sem=recv.at[sem],
            device_id=peer, device_id_type=MESH,
        )
        copy.start()
        sends.append(copy)
        return copy

    def got(ref, sem):
        pltpu.make_async_remote_copy(
            src_ref=ref, dst_ref=ref, send_sem=send.at[sem], recv_sem=recv.at[sem],
            device_id=core_peer, device_id_type=MESH,
        ).wait_recv()

    low = lax.broadcasted_iota(jnp.int32, (1, 128), 1) < 64
    sign = jnp.where(low, 1.0, -1.0).astype(F32)

    get_slices.wait()
    for j in range(2):
        for m in range(FREQ):
            both = fold_pair(
                m, lambda b: slices_raw[j, :, b * 128 : b * 128 + 128].astype(F32), low
            )
            fold_rows[m : m + 1, :128] = both[0:1]
            fold_rows[m : m + 1, 128:] = both[1:2]
        slices[0, j] = fold_rows[...].astype(BF16)

    def fold_images(first, count):
        def one(i, carry):
            for m in range(FREQ):
                both = fold_pair(
                    m, lambda b: images_raw[i, :, b * 128 : b * 128 + 128].astype(F32), low
                )
                row = pl.ds(m * 16 + i, 1)
                image_real[row, :] = both[0:1]
                image_imag[row, :] = both[1:2]
            return carry

        lax.fori_loop(first, first + count, one, 0)

    def image_half(cc):
        return pl.ds(pl.multiple_of(cc * 16, 16), 16)

    def send_images():
        def one(m):
            at = pl.ds(pl.multiple_of(m * 16, 16), 16)
            rows = jnp.concatenate([image_real[at, :], image_imag[at, :]], axis=1)
            images[m, image_half(c), :] = rows.astype(BF16)

        repeat(0, FREQ, one)
        here = images.at[:, image_half(c)]
        put(here, here, 0, core_peer)

    def fold_weight():
        for m in range(FREQ):
            row = fold_pair(m, lambda b: noise_weight[b : b + 1, :], low)
            if m == 0:
                weight[FREQ : FREQ + 1, :] = jnp.where(low, 0.0, row)
                row = jnp.where(low, row, 0.0)
            weight[m : m + 1, :] = row

    def count_cells():
        row = lax.broadcasted_iota(jnp.int32, (16, 128), 0)
        size = lax.broadcasted_iota(jnp.int32, (16, 128), 1) // IMGS
        total = jnp.zeros((16, 128), F32)
        for t in range(TRANS):
            shift_x, shift_y = shifts[0, t], shifts[1, t]
            at = jnp.where(shift_x >= 0, 3, 10) + shift_y
            hit = (row == at) & (size == jnp.abs(shift_x))
            total = total + jnp.where(hit, 1.0, 0.0)
        counts[...] = total

    def find_codes():
        block = targets[...]
        owner = (block * 43691) >> 17
        k = block - 3 * owner
        core_at, z_hi_at, x_at = (owner >> 4) & 1, (owner >> 5) & 3, owner >> 7
        y_at, z_lo_at = (owner >> 1) & 7, owner & 1
        code = (x_at * 2 + core_at) * 192 + k * 64 + (z_hi_at * 2 + z_lo_at) * 8 + y_at
        row = lax.broadcasted_iota(jnp.int32, (64, ORI), 0)
        mine = lax.broadcasted_iota(jnp.int32, (64, ORI), 1)
        x_from = (x + (mine >> 3)) & 3
        z_from = (zh + (mine >> 1)) & 3
        source = ((x_from * 4 + z_from) * 2 + c) * 2 + (mine & 1)
        pick = jnp.where(row == source, 1.0, 0.0).astype(BF16)
        dims = (((0,), (0,)), ((), ()))
        upper, lower = (code >> 5).astype(F32), (code & 31).astype(F32)
        upper = lax.dot_general(upper.astype(BF16), pick, dims, preferred_element_type=F32)
        lower = lax.dot_general(lower.astype(BF16), pick, dims, preferred_element_type=F32)
        code = upper * 32.0 + lower
        codes[...] = jnp.concatenate([code[16 * q : 16 * q + 16] for q in range(4)], axis=1)

    def choose(first, count):
        def one(t, carry):
            rows = lax.broadcasted_iota(jnp.int32, (128, 128), 0).astype(F32)
            rows = rows + (t * 128).astype(F32)
            at = pl.ds(pl.multiple_of(t * 128, 128), 128)
            for j in range(16):
                hit = rows == codes[j : j + 1, :]
                chosen[at, j * 128 : j * 128 + 128] = jnp.where(hit, 1.0, 0.0).astype(BF16)
            return carry

        lax.fori_loop(first, first + count, one, 0)

    def wait_images():
        got(images.at[:, image_half(1 - c)], 0)

    spread_images = jnp.where(
        lax.broadcasted_iota(jnp.int32, (2 * IMGS, 256), 0) % IMGS
        == lax.broadcasted_iota(jnp.int32, (2 * IMGS, 256), 1) % IMGS,
        1.0,
        0.0,
    ).astype(BF16)

    def align(first, count):
        def one(m):
            factors = trig[...] * weight[pl.ds(m, 1), :]
            rows = aligned_rows(images[lax.rem(m, FREQ)].astype(F32), factors)
            for r, row in enumerate(rows):
                high[m, r * IMGS : (r + 1) * IMGS, :] = row.astype(BF16)

        repeat(first, count, one)

    def align_turned(first, count):
        def one(m):
            w = weight[pl.ds(m, 1), :]
            pair = images[lax.rem(m, FREQ)].astype(F32) * jnp.concatenate([w, w], axis=1)
            top = pair.astype(BF16)
            terms = jnp.concatenate([top, (pair - top.astype(F32)).astype(BF16)], axis=0)
            turned = lax.dot_general(
                terms, spread_images, (((0,), (0,)), ((), ())), preferred_element_type=F32
            )
            turned = turned * trig_t[...]
            top = turned.astype(BF16)
            high_t[m] = top
            low_t[m] = (turned - top.astype(F32)).astype(BF16)

        repeat(first, count, one)

    def piece(dx, dz, h):
        return slices.at[dx * 4 + dz, :, pl.ds(h * 32, 32)]

    def single(dx, dz, h, j):
        return slices.at[dx * 4 + dz, j, pl.ds(h * 32, 32)]

    def gsem(kind, h):
        return 1 + kind * 2 + h

    z_up, z_down = z_peers[1], z_peers[5]

    def along_z(h):
        put(piece(0, 0, h), piece(0, 3, h), gsem(0, h), z_up)
        put(piece(0, 0, h), piece(0, 1, h), gsem(1, h), z_down)

    def along_x(dz, h):
        for s in range(1, 4):
            put(piece(0, dz, h), piece(4 - s, dz, h), gsem(3 + 3 * dz + s, h), x_peers[s - 1])

    def pass_z(h):
        got(piece(0, 3, h), gsem(0, h))
        put(single(0, 3, h, 0), single(0, 2, h, 0), gsem(2, h), z_up)
        got(piece(0, 1, h), gsem(1, h))
        put(single(0, 1, h, 1), single(0, 2, h, 1), gsem(3, h), z_down)

    def far_z(h):
        got(single(0, 2, h, 0), gsem(2, h))
        got(single(0, 2, h, 1), gsem(3, h))

    def got_x(h):
        for dz in (0, 3, 1, 2):
            for s in range(1, 4):
                got(piece(4 - s, dz, h), gsem(3 + 3 * dz + s, h))

    pl.semaphore_wait(barrier, len(everyone))
    for h in range(2):
        along_z(h)
        along_x(0, h)
    news = hear_of_y()
    next(news)
    get_images.wait()
    fold_images(0, 16)
    send_images()
    fold_weight()
    count_cells()
    pass_z(0)
    along_x(3, 0)
    along_x(1, 0)
    pass_z(1)
    along_x(3, 1)
    next(news)
    wait_images()
    get_trig_t.wait()
    align_turned(0, 16)
    far_z(0)
    along_x(2, 0)
    along_x(1, 1)
    far_z(1)
    along_x(2, 1)
    next(news)
    align_turned(16, STEPS - 16)
    next(news)
    get_sums.wait()

    acc[...] = jnp.zeros_like(acc)
    energy[...] = jnp.zeros_like(energy)

    def widen(h):
        def one(o):
            block = slices[o // 2, lax.rem(o, 2), pl.ds(h * 32, 32), :].astype(F32)
            rows = pl.ds(pl.multiple_of(o * FREQ + h * 32, 32), 32)
            real[rows, :] = block[:, :128]
            imag[rows, :] = block[:, 128:]

        repeat(0, ORI, one)

    def correlate(m, src):
        at = pl.ds(src, ORI, stride=FREQ)
        s_r, s_i = real[at, :], imag[at, :]
        energy[...] += weight[pl.ds(m, 1), :] * (s_r * s_r + s_i * s_i)
        left = jnp.concatenate(
            [
                jnp.concatenate([s_r, s_i], axis=1),
                jnp.concatenate([-sign * s_i, sign * s_r], axis=1),
            ],
            axis=0,
        ).astype(BF16)
        return jnp.dot(left, high_t[m], preferred_element_type=F32) + jnp.dot(
            left, low_t[m], preferred_element_type=F32
        )

    def add_scores(parts):
        for b in range(4):
            for k in range(2):
                for half in range(2):
                    even = k == half
                    if b == 0 and not even:
                        continue
                    lanes = slice(half * 128, half * 128 + 128)
                    total = acc[b, k * ORI : (k + 1) * ORI, lanes]
                    for m, value in parts:
                        value = value[k * ORI : (k + 1) * ORI, lanes]
                        if b:
                            value = value * sums[m, pl.ds(b if even else 4 + b, 1), :]
                        total = total + value
                    acc[b, k * ORI : (k + 1) * ORI, lanes] = total

    def score_half(h):
        widen(h)

        def some(group, carry):
            steps = [h * 32 + group * 8 + j for j in range(8)]
            add_scores([(m, correlate(m, m)) for m in steps])
            return carry

        lax.fori_loop(0, 4, some, 0)

    got_x(0)
    score_half(0)
    add_scores([(FREQ, correlate(FREQ, 0))])
    got_x(1)
    score_half(1)

    half_energy = 0.5 * jnp.sum(energy[...], axis=1, keepdims=True)
    peak = jnp.full((ORI, 128), -1e30, F32)
    for b in range(4):
        q1 = acc[b, :ORI, :128] - half_energy
        q2 = acc[b, :ORI, 128:]
        q4 = acc[b, ORI:, :128]
        q3 = acc[b, ORI:, 128:]
        for tau in (1, -1) if b else (1,):
            for sigma in (1, -1):
                entry = entry_of(sigma, tau * b)
                value = q1 - sigma * q3
                if b:
                    value = value - tau * (sigma * q2 + q4)
                expo[entry] = value
                live = counts[entry : entry + 1, :] > 0
                peak = jnp.maximum(peak, jnp.where(live, value, -1e30))
    peak = jnp.max(peak, axis=0, keepdims=True)
    peak = jnp.maximum(peak, pltpu.roll(peak, 32, 1))
    peak = jnp.maximum(peak, pltpu.roll(peak, 64, 1))
    mass = jnp.zeros((ORI, 128), F32)
    for entry in range(14):
        count = counts[entry : entry + 1, :]
        value = jnp.where(count > 0, expo[entry] - peak, -1e30)
        value = jnp.exp(value) * count
        expo[entry] = value
        mass = mass + value
    mass = jnp.sum(mass, axis=0, keepdims=True)
    mass = mass + pltpu.roll(mass, 32, 1)
    mass = mass + pltpu.roll(mass, 64, 1)
    own_peak = peak
    rest = jnp.zeros((6, 128), F32)
    stats_own[...] = jnp.concatenate([peak, mass, rest], axis=0)

    near = [put(stats_own, stats_near.at[s], 41 + s, near_peers[s]) for s in range(3)]
    for b in range(4):
        q1 = jnp.zeros((ORI, 128), F32)
        q2, q3, q4 = q1, q1, q1
        for tau in (1, -1) if b else (1,):
            for sigma in (1, -1):
                value = expo[entry_of(sigma, tau * b)]
                q1 = q1 + value
                q2 = q2 - (sigma * tau) * value
                q3 = q3 - sigma * value
                q4 = q4 - tau * value
        post[b, :ORI, :128] = q1
        post[b, :ORI, 128:] = q2
        post[b, ORI:, :128] = q4
        post[b, ORI:, 128:] = q3

    def spread(first, count):
        def one(m):
            for k in range(2):
                for half in range(2):
                    even = k == half
                    lanes = slice(half * 128, half * 128 + 128)
                    total = None
                    for b in range(4):
                        if b == 0 and not even:
                            continue
                        value = post[b, k * ORI : (k + 1) * ORI, lanes]
                        if b:
                            value = value * sums[m, pl.ds(b if even else 4 + b, 1), :]
                        total = value if total is None else total + value
                    back[m, k * ORI : (k + 1) * ORI, lanes] = total

        repeat(first, count, one, 4)

    spread(0, STEPS)
    find_codes()
    for copy in near:
        copy.wait_recv()
    peak, mass = merge_stats([stats_own[...]] + [stats_near[s] for s in range(3)])
    stats_mid[...] = jnp.concatenate([peak, mass, rest], axis=0)
    far = [put(stats_mid, stats_far.at[s], 44 + s, y_peers[s]) for s in range(7)]
    align(0, STEPS)
    choose(0, 12)
    for copy in far:
        copy.wait_recv()
    peak, mass = merge_stats([stats_mid[...]] + [stats_far[s] for s in range(7)])
    loglik = peak + jnp.log(mass)
    loglik_ref[...] = jnp.where(c == 0, loglik[:, :16], loglik[:, 16:32])
    scale = jnp.exp(own_peak - peak) / mass
    scale = jnp.concatenate([scale, scale], axis=1)

    def collect(m):
        grad = jnp.dot((back[m] * scale).astype(BF16), high[m], preferred_element_type=F32)
        out_real = grad[:ORI, :128] + sign * grad[ORI:, 128:]
        out_imag = grad[:ORI, 128:] - sign * grad[ORI:, :128]
        return jnp.concatenate([out_real, out_imag], axis=0)

    def insert(block, first, second):
        value = jnp.where(low, first, second)
        top = value.astype(BF16)
        left = jnp.concatenate([top, (value - top.astype(F32)).astype(BF16)], axis=0)
        out = jnp.dot(left, kernels[block], preferred_element_type=F32)
        out = out[: 2 * ORI] + out[2 * ORI :]
        at = lax.rem(block, 16) * 128 + (block // 16) * ORI
        rows = pl.ds(pl.multiple_of(at, ORI), ORI)
        inserted[rows, :] = jnp.concatenate([out[:ORI], out[ORI:]], axis=1).astype(BF16)

    def some_back(group, carry):
        for j in range(16):
            m = group * 16 + j
            folded[m] = collect(m)
        return carry

    lax.fori_loop(0, FREQ // 16, some_back, 0)
    folded[0] = folded[0] + collect(FREQ)
    get_kernels.wait()

    def some_insert(group, carry):
        for j in range(8):
            b = group * 8 + j
            insert(32 + b, folded[2 * b], pltpu.roll(folded[2 * b + 1], 64, 1))
            m = FREQ - 2 * b
            insert(b, pltpu.roll(folded[lax.rem(m, FREQ)], 64, 1), folded[m - 1])
        return carry

    lax.fori_loop(0, 4, some_insert, 0)

    def part_rows(xx, cc):
        return pl.ds(pl.multiple_of(xx * 384 + cc * 192, 192), 192)

    to_core = {}

    def scatter(s):
        xx = lax.rem(x + s, 4)
        rows = pl.ds(pl.multiple_of(xx * 384, 384), 384)
        part[rows, :] = jnp.dot(chosen[rows, :], inserted[...], preferred_element_type=F32)
        to_core[s] = put(part.at[part_rows(xx, 1 - c)], cores.at[s], 51 + s, core_peer)

    def both_cores(s):
        to_core[s].wait_recv()
        return part[part_rows(lax.rem(x + s, 4), c), :] + cores[s]

    steps = []

    def send_x(s):
        x_out[s - 1] = both_cores(s).astype(BF16)
        steps.append(put(x_out.at[s - 1], x_in.at[s - 1], 54 + s, x_peers[s - 1]))

    scatter(2)
    scatter(1)
    scatter(3)
    send_x(2)
    scatter(0)
    send_x(1)
    send_x(3)
    x_own[...] = both_cores(0)
    for copy in steps:
        copy.wait_recv()
    x_own[...] += sum(x_in[s].astype(F32) for s in range(3))
    for zz in range(8):
        rows = jnp.concatenate(
            [x_own[k * 64 + zz * 8 : k * 64 + zz * 8 + 8, :] for k in range(3)], axis=1
        )
        rows = jnp.concatenate([rows[:, :384], rows[:, 384:]], axis=0)
        z_own[zz] = rows
        z_out[zz] = rows.astype(BF16)
    steps = [
        put(z_out.at[lax.rem(z + s, 8)], z_in.at[s - 1], 57 + s, z_peers[s - 1])
        for s in range(1, 8)
    ]
    for copy in steps:
        copy.wait_recv()
    total = z_own[z]
    for s in range(7):
        total = total + z_in[s].astype(F32)
    for yy in range(8):
        for j in range(6):
            row = (j // 3) * 8 + yy
            y_out[yy, j : j + 1, :] = total[row : row + 1, (j % 3) * 128 : (j % 3) * 128 + 128]
        y_out[yy, 6:8, :] = jnp.zeros((2, 128), F32)
    steps = [
        put(y_out.at[lax.rem(y + s, 8)], y_in.at[s - 1], 64 + s, y_peers[s - 1])
        for s in range(1, 8)
    ]
    for copy in steps:
        copy.wait_recv()
    total = y_out[y]
    for s in range(7):
        total = total + y_in[s]
    for k in range(3):
        volume_ref[k] = total[2 * k : 2 * k + 2]
    for copy in sends:
        copy.wait_send()


def finish_kernel(volume, loglik, volume_ref, loglik_ref):
    volume_ref[...] = volume[...]
    loglik_ref[...] = loglik[...]


def shards(images, slices, noise_weight, shifts, kernels, targets):
    trig, sums = tables()
    trig_t = np.repeat(np.concatenate([trig, trig], axis=1).T, IMGS, axis=1)
    in_vmem = pl.BlockSpec(memory_space=pltpu.VMEM)
    in_smem = pl.BlockSpec(memory_space=pltpu.SMEM)
    anywhere = pl.BlockSpec(memory_space=pl.ANY)
    volume, loglik = pl.pallas_call(
        step_kernel,
        out_shape=(
            jax.ShapeDtypeStruct((3, 2, 128), F32),
            jax.ShapeDtypeStruct((1, 16), F32),
        ),
        in_specs=[
            anywhere, anywhere, in_vmem, in_smem, anywhere, in_vmem, in_vmem, anywhere, anywhere,
        ],
        out_specs=(in_vmem, in_vmem),
        scratch_shapes=[
            pltpu.VMEM((16, 2, PIX), BF16),
            pltpu.VMEM((2, 2, PIX), BF16),
            pltpu.VMEM((64, 128, 128), BF16),
            pltpu.VMEM((STEPS, 8, 128), F32),
            pltpu.VMEM((FREQ, 256), F32),
            pltpu.VMEM((FREQ * 16, 128), F32),
            pltpu.VMEM((FREQ * 16, 128), F32),
            pltpu.VMEM((FREQ, IMGS, 256), BF16),
            pltpu.VMEM((16, 2, FREQ, 256), BF16),
            pltpu.VMEM((72, 128), F32),
            pltpu.VMEM((256, 256), F32),
            pltpu.VMEM((STEPS, 256, 256), BF16),
            pltpu.VMEM((STEPS, 256, 256), BF16),
            pltpu.VMEM((STEPS, 256, 256), BF16),
            pltpu.VMEM((ORI * FREQ, 128), F32),
            pltpu.VMEM((ORI * FREQ, 128), F32),
            pltpu.VMEM((ORI, 128), F32),
            pltpu.VMEM((4, 2 * ORI, 256), F32),
            pltpu.VMEM((14, ORI, 128), F32),
            pltpu.VMEM((16, 128), F32),
            pltpu.VMEM((16, 128), F32),
            pltpu.VMEM((1536, 2048), BF16),
            pltpu.VMEM((4, 2 * ORI, 256), F32),
            pltpu.VMEM((STEPS, 2 * ORI, 256), F32),
            pltpu.VMEM((FREQ, 2 * ORI, 128), F32),
            pltpu.VMEM((FREQ * ORI, 256), BF16),
            pltpu.VMEM((1536, 256), F32),
            pltpu.VMEM((4, 192, 256), F32),
            pltpu.VMEM((8, 128), F32),
            pltpu.VMEM((3, 8, 128), F32),
            pltpu.VMEM((8, 128), F32),
            pltpu.VMEM((7, 8, 128), F32),
            pltpu.VMEM((3, 192, 256), BF16),
            pltpu.VMEM((3, 192, 256), BF16),
            pltpu.VMEM((192, 256), F32),
            pltpu.VMEM((8, 16, 384), BF16),
            pltpu.VMEM((7, 16, 384), BF16),
            pltpu.VMEM((8, 16, 384), F32),
            pltpu.VMEM((8, 8, 128), F32),
            pltpu.VMEM((7, 8, 128), F32),
            pltpu.SemaphoreType.DMA((72,)),
            pltpu.SemaphoreType.DMA((72,)),
            pltpu.SemaphoreType.DMA((5,)),
            pltpu.SemaphoreType.REGULAR((6,)),
        ],
        compiler_params=pltpu.CompilerParams(
            vmem_limit_bytes=VMEM_LIMIT, collective_id=0, has_side_effects=True
        ),
        name="expectation_step",
    )(
        images, slices, noise_weight.reshape(64, 128), shifts.T, kernels, targets,
        jnp.asarray(trig), jnp.asarray(sums), jnp.asarray(trig_t),
    )
    volume, loglik = pl.pallas_call(
        finish_kernel,
        out_shape=(
            jax.ShapeDtypeStruct((3, 2, 128), F32),
            jax.ShapeDtypeStruct((1, 16), F32),
        ),
        in_specs=[in_vmem, in_vmem],
        out_specs=(in_vmem, in_vmem),
        name="finish",
    )(volume, loglik)
    return volume, loglik.reshape(16)


def solution(mesh):
    placed = (
        P("dom", None, None),
        P(("orient", "dom"), None, None),
        P(),
        P(),
        P(),
        P("orient", None),
    )
    return jax.shard_map(
        shards,
        mesh=mesh,
        in_specs=placed,
        out_specs=(P(("dom", "orient"), None, None), P("dom")),
        check_vma=False,
    )
```

```python
import jax
import jax.numpy as jnp
import numpy as np
from jax import lax
from jax.experimental import pallas as pl
from jax.experimental.pallas import tpu as pltpu
from jax.sharding import PartitionSpec as P

F32 = jnp.float32
BF16 = jnp.bfloat16
MESH = pl.DeviceIdType.MESH
PIX = 8192
TRANS = 49
FREQ = 64
IMGS = 32
ORI = 32
STEPS = FREQ + 1
VMEM_LIMIT = 56 * 1024 * 1024


def tables():
    kx = np.arange(64)
    unit = 2.0 * np.pi / 128.0
    rows = np.zeros((8, 128), np.float32)
    for a in range(4):
        rows[a, :64] = rows[a, 64:] = np.cos(unit * a * kx)
    for a in range(1, 4):
        rows[4 + a, :64] = np.sin(unit * a * kx)
        rows[4 + a, 64:] = -np.sin(unit * a * kx)
    m = np.arange(STEPS)
    sums = np.zeros((STEPS, 8, 128), np.float32)
    for b in range(4):
        sums[:, b, :] = np.cos(unit * b * m)[:, None]
        sums[:, 4 + b, :] = np.where(m == 64, 0.0, np.sin(unit * b * m))[:, None]
    return rows, sums


def repeat(first, count, step, wide=8):
    def some(group, carry):
        for j in range(wide):
            step(first + group * wide + j)
        return carry

    lax.fori_loop(0, count // wide, some, 0)
    for j in range(count - count % wide, count):
        step(first + j)


def entry_of(sigma, shift_y):
    return (0 if sigma > 0 else 7) + shift_y + 3


def fold_pair(m, block, low):
    if m % 2 == 0:
        first = block(32 + m // 2)
        second = pltpu.roll(block(32 - m // 2 if m else 0), 64, 1)
    else:
        first = pltpu.roll(block(32 + (m - 1) // 2), 64, 1)
        second = block(32 - (m + 1) // 2)
    return jnp.where(low, first, second)


def aligned_rows(pair, factors):
    real, imag = pair[:, :128], pair[:, 128:]
    rows = []
    for r in range(8):
        row = factors[r : r + 1]
        if r == 4:
            rows.append(jnp.zeros((IMGS, 256), F32))
        else:
            rows.append(jnp.concatenate([real * row, imag * row], axis=1))
    return rows


def merge_stats(stats):
    peak = stats[0][0:1]
    for part in stats[1:]:
        peak = jnp.maximum(peak, part[0:1])
    mass = jnp.zeros_like(peak)
    for part in stats:
        mass = mass + part[1:2] * jnp.exp(part[0:1] - peak)
    return peak, mass


def step_kernel(
    images_hbm, slices_hbm, noise_weight, shifts, kernels_hbm, targets, trig, sums_hbm, trig_t_hbm,
    volume_ref, loglik_ref,
    images_raw, slices_raw, kernels, sums,
    fold_rows, image_real, image_imag, images, slices, weight, trig_t, high, high_t, low_t, real, imag, energy, acc, expo,
    counts, codes, chosen, post, back, folded, inserted, part, cores,
    stats_own, stats_near, stats_mid, stats_far,
    x_out, x_in, x_own, z_out, z_in, z_own, y_out, y_in,
    send, recv, local, heard,
):
    dom, ori = lax.axis_index("dom"), lax.axis_index("orient")
    c, zh, x = dom % 2, (dom // 2) % 4, dom // 8
    y, zl = ori // 2, ori % 2
    z = zh * 2 + zl

    def dev(dx, dz, dc, dy):
        xx, zz, yy = lax.rem(x + dx, 4), lax.rem(z + dz, 8), lax.rem(y + dy, 8)
        cc = 1 - c if dc else c
        return (xx * 8 + (zz // 2) * 2 + cc, yy * 2 + zz % 2)

    def dev_zl(dl, dc):
        cc = 1 - c if dc else c
        ll = 1 - zl if dl else zl
        return (x * 8 + zh * 2 + cc, y * 2 + ll)

    core_peer = dev(0, 0, 1, 0)
    x_peers = [dev(s, 0, 0, 0) for s in range(1, 4)]
    z_peers = [dev(0, s, 0, 0) for s in range(1, 8)]
    y_peers = [dev(0, 0, 0, s) for s in range(1, 8)]
    near_peers = [core_peer, dev_zl(1, 0), dev_zl(1, 1)]
    barrier = pltpu.get_barrier_semaphore()
    everyone = [core_peer, near_peers[1], z_peers[1], z_peers[5], y_peers[0], y_peers[6]]
    everyone += x_peers
    for peer in everyone:
        pl.semaphore_signal(barrier, inc=1, device_id=peer, device_id_type=MESH)

    get_slices = pltpu.make_async_copy(slices_hbm, slices_raw, local.at[0])
    get_slices.start()
    get_images = pltpu.make_async_copy(images_hbm, images_raw, local.at[1])
    get_images.start()
    get_kernels = pltpu.make_async_copy(kernels_hbm, kernels, local.at[2])
    get_kernels.start()
    get_sums = pltpu.make_async_copy(sums_hbm, sums, local.at[3])
    get_sums.start()
    get_trig_t = pltpu.make_async_copy(trig_t_hbm, trig_t, local.at[4])
    get_trig_t.start()

    def hear_of_y():
        for step in range(3):
            pl.semaphore_signal(
                heard.at[step], inc=1, device_id=y_peers[0], device_id_type=MESH
            )
            pl.semaphore_signal(
                heard.at[3 + step], inc=1, device_id=y_peers[6], device_id_type=MESH
            )
            yield
            pl.semaphore_wait(heard.at[step], 1)
            pl.semaphore_wait(heard.at[3 + step], 1)
        yield

    sends = []

    def put(src, dst, sem, peer):
        copy = pltpu.make_async_remote_copy(
            src_ref=src, dst_ref=dst, send_sem=send.at[sem], recv_sem=recv.at[sem],
            device_id=peer, device_id_type=MESH,
        )
        copy.start()
        sends.append(copy)
        return copy

    def got(ref, sem):
        pltpu.make_async_remote_copy(
            src_ref=ref, dst_ref=ref, send_sem=send.at[sem], recv_sem=recv.at[sem],
            device_id=core_peer, device_id_type=MESH,
        ).wait_recv()

    low = lax.broadcasted_iota(jnp.int32, (1, 128), 1) < 64
    sign = jnp.where(low, 1.0, -1.0).astype(F32)

    get_slices.wait()
    for j in range(2):
        for m in range(FREQ):
            both = fold_pair(
                m, lambda b: slices_raw[j, :, b * 128 : b * 128 + 128].astype(F32), low
            )
            fold_rows[m : m + 1, :128] = both[0:1]
            fold_rows[m : m + 1, 128:] = both[1:2]
        slices[0, j] = fold_rows[...].astype(BF16)

    def fold_images(first, count):
        def one(i, carry):
            for m in range(FREQ):
                both = fold_pair(
                    m, lambda b: images_raw[i, :, b * 128 : b * 128 + 128].astype(F32), low
                )
                row = pl.ds(m * 16 + i, 1)
                image_real[row, :] = both[0:1]
                image_imag[row, :] = both[1:2]
            return carry

        lax.fori_loop(first, first + count, one, 0)

    def image_half(cc):
        return pl.ds(pl.multiple_of(cc * 16, 16), 16)

    def send_images():
        def one(m):
            at = pl.ds(pl.multiple_of(m * 16, 16), 16)
            rows = jnp.concatenate([image_real[at, :], image_imag[at, :]], axis=1)
            images[m, image_half(c), :] = rows.astype(BF16)

        repeat(0, FREQ, one)
        here = images.at[:, image_half(c)]
        put(here, here, 0, core_peer)

    def fold_weight():
        for m in range(FREQ):
            row = fold_pair(m, lambda b: noise_weight[b : b + 1, :], low)
            if m == 0:
                weight[FREQ : FREQ + 1, :] = jnp.where(low, 0.0, row)
                row = jnp.where(low, row, 0.0)
            weight[m : m + 1, :] = row

    def count_cells():
        row = lax.broadcasted_iota(jnp.int32, (16, 128), 0)
        size = lax.broadcasted_iota(jnp.int32, (16, 128), 1) // IMGS
        total = jnp.zeros((16, 128), F32)
        for t in range(TRANS):
            shift_x, shift_y = shifts[0, t], shifts[1, t]
            at = jnp.where(shift_x >= 0, 3, 10) + shift_y
            hit = (row == at) & (size == jnp.abs(shift_x))
            total = total + jnp.where(hit, 1.0, 0.0)
        counts[...] = total

    def find_codes():
        block = targets[...]
        owner = (block * 43691) >> 17
        k = block - 3 * owner
        core_at, z_hi_at, x_at = (owner >> 4) & 1, (owner >> 5) & 3, owner >> 7
        y_at, z_lo_at = (owner >> 1) & 7, owner & 1
        code = (x_at * 2 + core_at) * 192 + k * 64 + (z_hi_at * 2 + z_lo_at) * 8 + y_at
        row = lax.broadcasted_iota(jnp.int32, (64, ORI), 0)
        mine = lax.broadcasted_iota(jnp.int32, (64, ORI), 1)
        x_from = (x + (mine >> 3)) & 3
        z_from = (zh + (mine >> 1)) & 3
        source = ((x_from * 4 + z_from) * 2 + c) * 2 + (mine & 1)
        pick = jnp.where(row == source, 1.0, 0.0).astype(BF16)
        dims = (((0,), (0,)), ((), ()))
        upper, lower = (code >> 5).astype(F32), (code & 31).astype(F32)
        upper = lax.dot_general(upper.astype(BF16), pick, dims, preferred_element_type=F32)
        lower = lax.dot_general(lower.astype(BF16), pick, dims, preferred_element_type=F32)
        code = upper * 32.0 + lower
        codes[...] = jnp.concatenate([code[16 * q : 16 * q + 16] for q in range(4)], axis=1)

    def choose(first, count):
        def one(t, carry):
            rows = lax.broadcasted_iota(jnp.int32, (128, 128), 0).astype(F32)
            rows = rows + (t * 128).astype(F32)
            at = pl.ds(pl.multiple_of(t * 128, 128), 128)
            for j in range(16):
                hit = rows == codes[j : j + 1, :]
                chosen[at, j * 128 : j * 128 + 128] = jnp.where(hit, 1.0, 0.0).astype(BF16)
            return carry

        lax.fori_loop(first, first + count, one, 0)

    def wait_images():
        got(images.at[:, image_half(1 - c)], 0)

    spread_images = jnp.where(
        lax.broadcasted_iota(jnp.int32, (2 * IMGS, 256), 0) % IMGS
        == lax.broadcasted_iota(jnp.int32, (2 * IMGS, 256), 1) % IMGS,
        1.0,
        0.0,
    ).astype(BF16)

    def align(first, count):
        def one(m):
            factors = trig[...] * weight[pl.ds(m, 1), :]
            rows = aligned_rows(images[lax.rem(m, FREQ)].astype(F32), factors)
            for r, row in enumerate(rows):
                high[m, r * IMGS : (r + 1) * IMGS, :] = row.astype(BF16)

        repeat(first, count, one)

    def align_turned(first, count):
        def one(m):
            w = weight[pl.ds(m, 1), :]
            pair = images[lax.rem(m, FREQ)].astype(F32) * jnp.concatenate([w, w], axis=1)
            top = pair.astype(BF16)
            terms = jnp.concatenate([top, (pair - top.astype(F32)).astype(BF16)], axis=0)
            turned = lax.dot_general(
                terms, spread_images, (((0,), (0,)), ((), ())), preferred_element_type=F32
            )
            turned = turned * trig_t[...]
            top = turned.astype(BF16)
            high_t[m] = top
            low_t[m] = (turned - top.astype(F32)).astype(BF16)

        repeat(first, count, one)

    def piece(dx, dz, h):
        return slices.at[dx * 4 + dz, :, pl.ds(h * 32, 32)]

    def single(dx, dz, h, j):
        return slices.at[dx * 4 + dz, j, pl.ds(h * 32, 32)]

    def gsem(kind, h):
        return 1 + kind * 2 + h

    z_up, z_down = z_peers[1], z_peers[5]

    def along_z(h):
        put(piece(0, 0, h), piece(0, 3, h), gsem(0, h), z_up)
        put(piece(0, 0, h), piece(0, 1, h), gsem(1, h), z_down)

    def along_x(dz, h):
        for s in range(1, 4):
            put(piece(0, dz, h), piece(4 - s, dz, h), gsem(3 + 3 * dz + s, h), x_peers[s - 1])

    def pass_z(h):
        got(piece(0, 3, h), gsem(0, h))
        put(single(0, 3, h, 0), single(0, 2, h, 0), gsem(2, h), z_up)
        got(piece(0, 1, h), gsem(1, h))
        put(single(0, 1, h, 1), single(0, 2, h, 1), gsem(3, h), z_down)

    def far_z(h):
        got(single(0, 2, h, 0), gsem(2, h))
        got(single(0, 2, h, 1), gsem(3, h))

    def got_x(h):
        for dz in (0, 3, 1, 2):
            for s in range(1, 4):
                got(piece(4 - s, dz, h), gsem(3 + 3 * dz + s, h))

    pl.semaphore_wait(barrier, len(everyone))
    for h in range(2):
        along_z(h)
        along_x(0, h)
    news = hear_of_y()
    next(news)
    get_images.wait()
    fold_images(0, 16)
    send_images()
    fold_weight()
    count_cells()
    pass_z(0)
    along_x(3, 0)
    along_x(1, 0)
    pass_z(1)
    along_x(3, 1)
    next(news)
    wait_images()
    get_trig_t.wait()
    align_turned(0, 16)
    far_z(0)
    along_x(2, 0)
    along_x(1, 1)
    far_z(1)
    along_x(2, 1)
    next(news)
    align_turned(16, STEPS - 16)
    next(news)
    get_sums.wait()

    acc[...] = jnp.zeros_like(acc)
    energy[...] = jnp.zeros_like(energy)

    def widen(h):
        def one(o):
            block = slices[o // 2, lax.rem(o, 2), pl.ds(h * 32, 32), :].astype(F32)
            rows = pl.ds(pl.multiple_of(o * FREQ + h * 32, 32), 32)
            real[rows, :] = block[:, :128]
            imag[rows, :] = block[:, 128:]

        repeat(0, ORI, one)

    def correlate(m, src):
        at = pl.ds(src, ORI, stride=FREQ)
        s_r, s_i = real[at, :], imag[at, :]
        energy[...] += weight[pl.ds(m, 1), :] * (s_r * s_r + s_i * s_i)
        left = jnp.concatenate(
            [
                jnp.concatenate([s_r, s_i], axis=1),
                jnp.concatenate([-sign * s_i, sign * s_r], axis=1),
            ],
            axis=0,
        ).astype(BF16)
        return jnp.dot(left, high_t[m], preferred_element_type=F32) + jnp.dot(
            left, low_t[m], preferred_element_type=F32
        )

    def add_scores(parts):
        for b in range(4):
            for k in range(2):
                for half in range(2):
                    even = k == half
                    if b == 0 and not even:
                        continue
                    lanes = slice(half * 128, half * 128 + 128)
                    total = acc[b, k * ORI : (k + 1) * ORI, lanes]
                    for m, value in parts:
                        value = value[k * ORI : (k + 1) * ORI, lanes]
                        if b:
                            value = value * sums[m, pl.ds(b if even else 4 + b, 1), :]
                        total = total + value
                    acc[b, k * ORI : (k + 1) * ORI, lanes] = total

    def score_half(h):
        widen(h)

        def some(group, carry):
            steps = [h * 32 + group * 16 + j for j in range(16)]
            add_scores([(m, correlate(m, m)) for m in steps])
            return carry

        lax.fori_loop(0, 2, some, 0)

    got_x(0)
    score_half(0)
    add_scores([(FREQ, correlate(FREQ, 0))])
    got_x(1)
    score_half(1)

    half_energy = 0.5 * jnp.sum(energy[...], axis=1, keepdims=True)
    peak = jnp.full((ORI, 128), -1e30, F32)
    for b in range(4):
        q1 = acc[b, :ORI, :128] - half_energy
        q2 = acc[b, :ORI, 128:]
        q4 = acc[b, ORI:, :128]
        q3 = acc[b, ORI:, 128:]
        for tau in (1, -1) if b else (1,):
            for sigma in (1, -1):
                entry = entry_of(sigma, tau * b)
                value = q1 - sigma * q3
                if b:
                    value = value - tau * (sigma * q2 + q4)
                expo[entry] = value
                live = counts[entry : entry + 1, :] > 0
                peak = jnp.maximum(peak, jnp.where(live, value, -1e30))
    peak = jnp.max(peak, axis=0, keepdims=True)
    peak = jnp.maximum(peak, pltpu.roll(peak, 32, 1))
    peak = jnp.maximum(peak, pltpu.roll(peak, 64, 1))
    mass = jnp.zeros((ORI, 128), F32)
    for entry in range(14):
        count = counts[entry : entry + 1, :]
        value = jnp.where(count > 0, expo[entry] - peak, -1e30)
        value = jnp.exp(value) * count
        expo[entry] = value
        mass = mass + value
    mass = jnp.sum(mass, axis=0, keepdims=True)
    mass = mass + pltpu.roll(mass, 32, 1)
    mass = mass + pltpu.roll(mass, 64, 1)
    own_peak = peak
    rest = jnp.zeros((6, 128), F32)
    stats_own[...] = jnp.concatenate([peak, mass, rest], axis=0)

    near = [put(stats_own, stats_near.at[s], 41 + s, near_peers[s]) for s in range(3)]
    for b in range(4):
        q1 = jnp.zeros((ORI, 128), F32)
        q2, q3, q4 = q1, q1, q1
        for tau in (1, -1) if b else (1,):
            for sigma in (1, -1):
                value = expo[entry_of(sigma, tau * b)]
                q1 = q1 + value
                q2 = q2 - (sigma * tau) * value
                q3 = q3 - sigma * value
                q4 = q4 - tau * value
        post[b, :ORI, :128] = q1
        post[b, :ORI, 128:] = q2
        post[b, ORI:, :128] = q4
        post[b, ORI:, 128:] = q3

    def spread(first, count):
        def one(m):
            for k in range(2):
                for half in range(2):
                    even = k == half
                    lanes = slice(half * 128, half * 128 + 128)
                    total = None
                    for b in range(4):
                        if b == 0 and not even:
                            continue
                        value = post[b, k * ORI : (k + 1) * ORI, lanes]
                        if b:
                            value = value * sums[m, pl.ds(b if even else 4 + b, 1), :]
                        total = value if total is None else total + value
                    back[m, k * ORI : (k + 1) * ORI, lanes] = total

        repeat(first, count, one, 4)

    spread(0, STEPS)
    find_codes()
    for copy in near:
        copy.wait_recv()
    peak, mass = merge_stats([stats_own[...]] + [stats_near[s] for s in range(3)])
    stats_mid[...] = jnp.concatenate([peak, mass, rest], axis=0)
    far = [put(stats_mid, stats_far.at[s], 44 + s, y_peers[s]) for s in range(7)]
    align(0, STEPS)
    choose(0, 12)
    for copy in far:
        copy.wait_recv()
    peak, mass = merge_stats([stats_mid[...]] + [stats_far[s] for s in range(7)])
    loglik = peak + jnp.log(mass)
    loglik_ref[...] = jnp.where(c == 0, loglik[:, :16], loglik[:, 16:32])
    scale = jnp.exp(own_peak - peak) / mass
    scale = jnp.concatenate([scale, scale], axis=1)

    def collect(m):
        grad = jnp.dot((back[m] * scale).astype(BF16), high[m], preferred_element_type=F32)
        out_real = grad[:ORI, :128] + sign * grad[ORI:, 128:]
        out_imag = grad[:ORI, 128:] - sign * grad[ORI:, :128]
        return jnp.concatenate([out_real, out_imag], axis=0)

    def insert(block, first, second):
        value = jnp.where(low, first, second)
        top = value.astype(BF16)
        left = jnp.concatenate([top, (value - top.astype(F32)).astype(BF16)], axis=0)
        out = jnp.dot(left, kernels[block], preferred_element_type=F32)
        out = out[: 2 * ORI] + out[2 * ORI :]
        at = lax.rem(block, 16) * 128 + (block // 16) * ORI
        rows = pl.ds(pl.multiple_of(at, ORI), ORI)
        inserted[rows, :] = jnp.concatenate([out[:ORI], out[ORI:]], axis=1).astype(BF16)

    def some_back(group, carry):
        for j in range(16):
            m = group * 16 + j
            folded[m] = collect(m)
        return carry

    lax.fori_loop(0, FREQ // 16, some_back, 0)
    folded[0] = folded[0] + collect(FREQ)
    get_kernels.wait()

    def some_insert(group, carry):
        for j in range(8):
            b = group * 8 + j
            insert(32 + b, folded[2 * b], pltpu.roll(folded[2 * b + 1], 64, 1))
            m = FREQ - 2 * b
            insert(b, pltpu.roll(folded[lax.rem(m, FREQ)], 64, 1), folded[m - 1])
        return carry

    lax.fori_loop(0, 4, some_insert, 0)

    def part_rows(xx, cc):
        return pl.ds(pl.multiple_of(xx * 384 + cc * 192, 192), 192)

    to_core = {}

    def scatter(s, cc):
        rows = part_rows(lax.rem(x + s, 4), cc)
        part[rows, :] = jnp.dot(chosen[rows, :], inserted[...], preferred_element_type=F32)

    def scatter_other(s):
        scatter(s, 1 - c)
        to_core[s] = put(
            part.at[part_rows(lax.rem(x + s, 4), 1 - c)], cores.at[s], 51 + s, core_peer
        )

    def both_cores(s):
        to_core[s].wait_recv()
        return part[part_rows(lax.rem(x + s, 4), c), :] + cores[s]

    steps = []

    def send_x(s):
        x_out[s - 1] = both_cores(s).astype(BF16)
        steps.append(put(x_out.at[s - 1], x_in.at[s - 1], 54 + s, x_peers[s - 1]))

    for s in (2, 1, 3):
        scatter_other(s)
    for s in (2, 1, 3):
        scatter(s, c)
        send_x(s)
    scatter_other(0)
    scatter(0, c)
    x_own[...] = both_cores(0)
    for copy in steps:
        copy.wait_recv()
    x_own[...] += sum(x_in[s].astype(F32) for s in range(3))
    def z_chunk(zz):
        rows = jnp.concatenate(
            [x_own[pl.ds(pl.multiple_of(k * 64 + zz * 8, 8), 8), :] for k in range(3)], axis=1
        )
        return jnp.concatenate([rows[:, :384], rows[:, 384:]], axis=0)

    steps = []
    for s in (4, 3, 5, 2, 6, 1, 7):
        z_out[s - 1] = z_chunk(lax.rem(z + s, 8)).astype(BF16)
        steps.append(put(z_out.at[s - 1], z_in.at[s - 1], 57 + s, z_peers[s - 1]))
    z_own[...] = z_chunk(z)
    for copy in steps:
        copy.wait_recv()
    total = z_own[...]
    for s in range(7):
        total = total + z_in[s].astype(F32)
    for yy in range(8):
        for j in range(6):
            row = (j // 3) * 8 + yy
            y_out[yy, j : j + 1, :] = total[row : row + 1, (j % 3) * 128 : (j % 3) * 128 + 128]
        y_out[yy, 6:8, :] = jnp.zeros((2, 128), F32)
    steps = [
        put(y_out.at[lax.rem(y + s, 8)], y_in.at[s - 1], 64 + s, y_peers[s - 1])
        for s in range(1, 8)
    ]
    for copy in steps:
        copy.wait_recv()
    total = y_out[y]
    for s in range(7):
        total = total + y_in[s]
    for k in range(3):
        volume_ref[k] = total[2 * k : 2 * k + 2]
    for copy in sends:
        copy.wait_send()


def finish_kernel(volume, loglik, volume_ref, loglik_ref):
    volume_ref[...] = volume[...]
    loglik_ref[...] = loglik[...]


def shards(images, slices, noise_weight, shifts, kernels, targets):
    trig, sums = tables()
    trig_t = np.repeat(np.concatenate([trig, trig], axis=1).T, IMGS, axis=1)
    in_vmem = pl.BlockSpec(memory_space=pltpu.VMEM)
    in_smem = pl.BlockSpec(memory_space=pltpu.SMEM)
    anywhere = pl.BlockSpec(memory_space=pl.ANY)
    volume, loglik = pl.pallas_call(
        step_kernel,
        out_shape=(
            jax.ShapeDtypeStruct((3, 2, 128), F32),
            jax.ShapeDtypeStruct((1, 16), F32),
        ),
        in_specs=[
            anywhere, anywhere, in_vmem, in_smem, anywhere, in_vmem, in_vmem, anywhere, anywhere,
        ],
        out_specs=(in_vmem, in_vmem),
        scratch_shapes=[
            pltpu.VMEM((16, 2, PIX), BF16),
            pltpu.VMEM((2, 2, PIX), BF16),
            pltpu.VMEM((64, 128, 128), BF16),
            pltpu.VMEM((STEPS, 8, 128), F32),
            pltpu.VMEM((FREQ, 256), F32),
            pltpu.VMEM((FREQ * 16, 128), F32),
            pltpu.VMEM((FREQ * 16, 128), F32),
            pltpu.VMEM((FREQ, IMGS, 256), BF16),
            pltpu.VMEM((16, 2, FREQ, 256), BF16),
            pltpu.VMEM((72, 128), F32),
            pltpu.VMEM((256, 256), F32),
            pltpu.VMEM((STEPS, 256, 256), BF16),
            pltpu.VMEM((STEPS, 256, 256), BF16),
            pltpu.VMEM((STEPS, 256, 256), BF16),
            pltpu.VMEM((ORI * FREQ, 128), F32),
            pltpu.VMEM((ORI * FREQ, 128), F32),
            pltpu.VMEM((ORI, 128), F32),
            pltpu.VMEM((4, 2 * ORI, 256), F32),
            pltpu.VMEM((14, ORI, 128), F32),
            pltpu.VMEM((16, 128), F32),
            pltpu.VMEM((16, 128), F32),
            pltpu.VMEM((1536, 2048), BF16),
            pltpu.VMEM((4, 2 * ORI, 256), F32),
            pltpu.VMEM((STEPS, 2 * ORI, 256), F32),
            pltpu.VMEM((FREQ, 2 * ORI, 128), F32),
            pltpu.VMEM((FREQ * ORI, 256), BF16),
            pltpu.VMEM((1536, 256), F32),
            pltpu.VMEM((4, 192, 256), F32),
            pltpu.VMEM((8, 128), F32),
            pltpu.VMEM((3, 8, 128), F32),
            pltpu.VMEM((8, 128), F32),
            pltpu.VMEM((7, 8, 128), F32),
            pltpu.VMEM((3, 192, 256), BF16),
            pltpu.VMEM((3, 192, 256), BF16),
            pltpu.VMEM((192, 256), F32),
            pltpu.VMEM((7, 16, 384), BF16),
            pltpu.VMEM((7, 16, 384), BF16),
            pltpu.VMEM((16, 384), F32),
            pltpu.VMEM((8, 8, 128), F32),
            pltpu.VMEM((7, 8, 128), F32),
            pltpu.SemaphoreType.DMA((72,)),
            pltpu.SemaphoreType.DMA((72,)),
            pltpu.SemaphoreType.DMA((5,)),
            pltpu.SemaphoreType.REGULAR((6,)),
        ],
        compiler_params=pltpu.CompilerParams(
            vmem_limit_bytes=VMEM_LIMIT, collective_id=0, has_side_effects=True
        ),
        name="expectation_step",
    )(
        images, slices, noise_weight.reshape(64, 128), shifts.T, kernels, targets,
        jnp.asarray(trig), jnp.asarray(sums), jnp.asarray(trig_t),
    )
    volume, loglik = pl.pallas_call(
        finish_kernel,
        out_shape=(
            jax.ShapeDtypeStruct((3, 2, 128), F32),
            jax.ShapeDtypeStruct((1, 16), F32),
        ),
        in_specs=[in_vmem, in_vmem],
        out_specs=(in_vmem, in_vmem),
        name="finish",
    )(volume, loglik)
    return volume, loglik.reshape(16)


def solution(mesh):
    placed = (
        P("dom", None, None),
        P(("orient", "dom"), None, None),
        P(),
        P(),
        P(),
        P("orient", None),
    )
    return jax.shard_map(
        shards,
        mesh=mesh,
        in_specs=placed,
        out_specs=(P(("dom", "orient"), None, None), P("dom")),
        check_vma=False,
    )
```
